512 devices in a mesh: frame: 16 (over x, z_lo), height: 16 (over y, core), cand: 2 (over z_hi).
Axes of the slice: x: 4, y: 8, z: 8 (z_hi: 2, z_lo: 4; z = z_hi * 4 + z_lo), core: 2. Of those that a mesh axis runs over, the one named last changes fastest.
Arguments:
- queries: bfloat16 [64, 64, 16, 1536], P(('cand', 'frame'), 'height'), parts along dimension 0, may hold values from -6 to 6
- key_value: bfloat16 [2, 64, 64, 16, 1536], P(None, ('cand', 'frame'), 'height'), parts along dimension 1, may hold values from -6 to 6
- windows: int32 [12, 3], replicated, may hold values from 0 to 1, as said below
Outputs:
- attended: bfloat16 [64, 64, 16, 1536], P(('cand', 'frame'), 'height'), parts along dimension 0
The draws below stay inside these ranges and needn't reach their ends.
There are 2 independent parts, one for each index of `cand`. The reference program is written for one: setup_inputs(seed, part) draws one part's arguments, and reference() takes and returns one part's arrays. A program takes and returns all parts, laid end to end along the dimension named above; an argument that names none is the same for every part. Nothing has to cross between parts.
Inputs may be any that keep to these rules, and one draw needn't show every extreme that they name: `windows`: column 0 is at most 1, column 1 at most 1, column 2 at most 1; each column reaches its most for some head and 0 for another.
All inputs are finite; a program needn't handle non-finite values.
Results may differ from the reference program's by a relative error of at most 0.0046.
Values may be sent and summed in bfloat16 or wider, within the bound.
A program may use at most 64 MiB of HBM per device.

```python
import math
import jax
import jax.numpy as jnp
from jax import lax

HEADS = 12
HD = 128
CF = 2
CH = 4
W = 16
TF = 2
TH = 8
TW = 8
WF_MAX = 1
WH_MAX = 1
WW_MAX = 1
KF = 6
KH = 24
FRAMES = 32
ROWS = 64
N_FRAME = 16
N_HEIGHT = 16


def draw_queries(key, part):
    grid_shape = (FRAMES, ROWS, W, HEADS * HD)
    key = jax.random.fold_in(key, 3)
    return jnp.clip(jax.random.normal(key, grid_shape, jnp.float32), -5.0, 5.0).astype(jnp.bfloat16)


def draw_key_value(key, part):
    grid_shape = (FRAMES, ROWS, W, HEADS * HD)
    key = jax.random.fold_in(key, 4)
    return jnp.clip(jax.random.normal(key, (2,) + grid_shape, jnp.float32), -5.0, 5.0).astype(jnp.bfloat16)


def draw_windows(key, part):
    key = jax.random.fold_in(key, 5)
    upper = jnp.array([WF_MAX, WH_MAX, WW_MAX], jnp.int32)
    raw_draw = jax.random.randint(jax.random.fold_in(key, 1), (HEADS, 3), 0, 1048576) % (upper[None, :] + 1)
    widest = jax.random.randint(jax.random.fold_in(key, 2), (3,), 0, HEADS)
    narrow = (widest + 1) % HEADS
    head_ids = lax.broadcasted_iota(jnp.int32, (HEADS, 3), 0)
    shaped = jnp.where(head_ids == narrow[None, :], 0, raw_draw)
    return jnp.where(head_ids == widest[None, :], upper[None, :], shaped).astype(jnp.int32)


def setup_inputs(seed: int = 0, part: int = 0) -> dict:
    keys = jax.random.split(jax.random.key(seed), 4)
    own_keys = jax.random.split(jax.random.fold_in(keys[3], part), 4)
    return {
        "queries": draw_queries(jax.random.fold_in(jax.random.fold_in(keys[3], part), 71), part),
        "key_value": draw_key_value(jax.random.fold_in(jax.random.fold_in(keys[3], part), 71), part),
        "windows": draw_windows(jax.random.fold_in(keys[3], 71), part),
    }


def positions(frame_start, frame_count, row_start, row_count, columns):
    grid_shape = (frame_count, row_count, columns)
    frame_ids = frame_start + lax.broadcasted_iota(jnp.int32, grid_shape, 0)
    row_ids = row_start + lax.broadcasted_iota(jnp.int32, grid_shape, 1)
    column_ids = lax.broadcasted_iota(jnp.int32, grid_shape, 2)
    return (frame_ids.reshape(-1), row_ids.reshape(-1), column_ids.reshape(-1))

def within(key_pos):
    return (key_pos[0] >= 0) & (key_pos[0] < FRAMES) & (key_pos[1] >= 0) & (key_pos[1] < ROWS)

def allowed(query_pos, key_pos, inside_grid, windows):
    result = inside_grid[None, None, :]
    for dimension, extent in enumerate((TF, TH, TW)):
        distance = jnp.abs(query_pos[dimension][:, None] // extent - key_pos[dimension][None, :] // extent)
        result = result & (distance[None] <= windows[:, dimension][:, None, None])
    return result

def attend(queries_block, keys_block, values_block, query_pos, key_pos, inside_grid, windows):
    scaling = 1.0 / math.sqrt(queries_block.shape[-1])
    scores = jnp.einsum('qhd,khd->hqk', queries_block.astype(jnp.float32), keys_block.astype(jnp.float32)) * scaling
    permitted = allowed(query_pos, key_pos, inside_grid, windows)
    masked = jnp.where(permitted, scores, -jnp.inf)
    largest = lax.optimization_barrier(jnp.max(masked, axis=-1, keepdims=True))
    exponentials = jnp.exp(masked - largest)
    totals = lax.optimization_barrier(jnp.sum(exponentials, axis=-1))
    weights = exponentials.astype(jnp.bfloat16)
    blended = jnp.einsum('hqk,khd->qhd', weights.astype(jnp.float32), values_block.astype(jnp.float32))
    return (blended / jnp.transpose(totals)[:, :, None]).astype(jnp.bfloat16)

def reference(queries, key_value, windows):
    pad_frames = WF_MAX * TF
    pad_rows = WH_MAX * TH
    padded = jnp.pad(key_value, ((0, 0), (pad_frames, pad_frames), (pad_rows, pad_rows), (0, 0), (0, 0)))
    features = HEADS * HD

    def one_block(block_index):
        frame_start = block_index // N_HEIGHT * CF
        row_start = block_index % N_HEIGHT * CH
        key_frame_start = frame_start // TF * TF - pad_frames
        key_row_start = row_start // TH * TH - pad_rows
        zero_index = jnp.zeros((), jnp.int32)
        block_queries = lax.dynamic_slice(queries, (frame_start, row_start, zero_index, zero_index), (CF, CH, W, features))
        block_pairs = lax.dynamic_slice(padded, (zero_index, key_frame_start + pad_frames, key_row_start + pad_rows, zero_index, zero_index), (2, KF, KH, W, features))
        query_pos = positions(frame_start, CF, row_start, CH, W)
        key_pos = positions(key_frame_start, KF, key_row_start, KH, W)
        result = attend(block_queries.reshape(-1, HEADS, HD), block_pairs[0].reshape(-1, HEADS, HD), block_pairs[1].reshape(-1, HEADS, HD), query_pos, key_pos, within(key_pos), windows)
        return result.reshape(CF, CH, W, features)
    blocks = lax.map(one_block, jnp.arange(N_FRAME * N_HEIGHT, dtype=jnp.int32))
    arranged = blocks.reshape(N_FRAME, N_HEIGHT, CF, CH, W, features).transpose(0, 2, 1, 3, 4, 5)
    return arranged.reshape(FRAMES, ROWS, W, features)
```

```python
import functools
import math

import jax
import jax.numpy as jnp
from jax import lax
from jax.experimental import pallas as pl
from jax.experimental.pallas import tpu as pltpu
from jax.sharding import PartitionSpec as P

HEADS = 12
HALF = HEADS // 2
HD = 128
TOK = 128
CHIP = 2 * TOK
W = 16
TW = 8
NEG = -1e30
SCALE = math.log2(math.e) / math.sqrt(HD)
MESH = pl.DeviceIdType.MESH


def dot(a, b, dims):
    return lax.dot_general(a, b, ((dims[0], dims[1]), ((), ())), preferred_element_type=jnp.float32)


PLANS = ((4, 0, 12), (5, 0, 12), (6, 0, 12), (7, 0, 12), (8, 0, 12), (12, 0, 12))


def sort_kernel(q, kv, win, packed, flags, choice):
    keys, tall, wide, lone = [], jnp.int32(0), jnp.int32(0), jnp.int32(0)
    for h in range(HEADS):
        wf, wh = jnp.minimum(win[h, 0], 1), jnp.minimum(win[h, 1], 1)
        keys.append((3 - 3 * wf - wh + 2 * wf * wh) * 16 + h)
        wide = wide + wf
        tall = tall + wh
        lone = lone + wf * (1 - wh)
    ranks = []
    for h in range(HEADS):
        rank = jnp.int32(0)
        for k in range(HEADS):
            if k != h:
                rank = rank + jnp.where(keys[k] < keys[h], 1, 0)
        ranks.append(rank)
    for s in range(HEADS):
        head = jnp.int32(0)
        for h in range(HEADS):
            head = head + jnp.where(ranks[h] == s, h, 0)
        for i in range(3):
            flags[s, i] = win[head, i]
        flags[s, 3] = ranks[s]
        col = pl.multiple_of(head * HD, HD)
        packed[s, 0] = kv[0, :, pl.ds(col, HD)]
        packed[s, 1] = kv[1, :, pl.ds(col, HD)].T
        packed[s, 2] = q[:, pl.ds(col, HD)]
    best = jnp.int32(len(PLANS) - 1)
    for i in reversed(range(len(PLANS) - 1)):
        nf, h0, h1 = PLANS[i]
        best = jnp.where((wide <= nf) & (lone >= h0) & (lone + tall <= h1), i, best)
    choice[0] = best


def place_kernel(o, flags, out):
    for h in range(HEADS):
        out[:, h * HD : (h + 1) * HD] = o[flags[h, 3]]


def kernel(
    cfg,
    n_frame,
    n_chip_y,
    packed,
    flags,
    out,
    own,
    nb,
    qn,
    acc,
    ml,
    rs,
    rr,
    oh,
    own_l,
    own_s,
    own_r,
    z_s,
    z_r,
    q_s,
    q_r,
    ret_s,
    ret_r,
    o_l,
    o_s,
    o_r,
):
    nf, h0, h1 = cfg
    f = lax.axis_index("frame")
    height = lax.axis_index("height")
    y = height // 2
    c = height % 2
    other = 1 - c
    z_ok = (f > 0, f < n_frame - 1)
    y_ok = (y > 0, y < n_chip_y - 1)
    z_dev = (f - 1, f + 1)
    y_dev = (y - 1, y + 1)
    partner = {"height": 2 * y + other}

    barrier = pltpu.get_barrier_semaphore()
    pl.semaphore_signal(barrier, inc=1, device_id=partner, device_id_type=MESH)
    for d in range(2):

        @pl.when(z_ok[d])
        def _():
            for g in range(2):
                pl.semaphore_signal(
                    barrier,
                    inc=1,
                    device_id={"frame": z_dev[d], "height": 2 * y + g},
                    device_id_type=MESH,
                )

        @pl.when(y_ok[d])
        def _():
            for g in range(2):
                pl.semaphore_signal(
                    barrier,
                    inc=1,
                    device_id={"height": 2 * y_dev[d] + g},
                    device_id_type=MESH,
                )

    def own_load(j):
        return pltpu.make_async_copy(packed.at[2 * j + c], own.at[j, c], own_l.at[j])

    @pl.loop(0, HALF)
    def _(j):
        own_load(j).start()

    for d in range(2):

        @pl.when(jnp.logical_not(y_ok[d]))
        def _():
            rr[d] = jnp.zeros(rr.shape[1:], rr.dtype)

    pl.semaphore_wait(
        barrier,
        1
        + 2 * sum(jnp.where(ok, 1, 0) for ok in z_ok)
        + 2 * sum(jnp.where(ok, 1, 0) for ok in y_ok),
    )

    def z_copy(d, j, mine):
        g = c if mine else other
        return pltpu.make_async_remote_copy(
            src_ref=packed.at[2 * j + g, pl.ds(0, 2)],
            dst_ref=nb.at[1 - d, j, c],
            send_sem=z_s.at[d, j, 0 if mine else 1],
            recv_sem=z_r.at[1 - d, j, c],
            device_id={"frame": z_dev[d], "height": 2 * y + g},
            device_id_type=MESH,
        )

    def q_copy(d, j, mine):
        g = c if mine else other
        return pltpu.make_async_remote_copy(
            src_ref=packed.at[2 * j + g, 2],
            dst_ref=qn.at[1 - d, j, c],
            send_sem=q_s.at[d, j, 0 if mine else 1],
            recv_sem=q_r.at[1 - d, j, c],
            device_id={"height": 2 * y_dev[d] + g},
            device_id_type=MESH,
        )

    def own_copy(j):
        return pltpu.make_async_remote_copy(
            src_ref=packed.at[2 * j + other],
            dst_ref=own.at[j, c],
            send_sem=own_s.at[j],
            recv_sem=own_r.at[j],
            device_id=partner,
            device_id_type=MESH,
        )

    def ret_copy(d, j):
        return pltpu.make_async_remote_copy(
            src_ref=rs.at[d, j],
            dst_ref=rr.at[1 - d, j],
            send_sem=ret_s.at[d, j],
            recv_sem=ret_r.at[1 - d, j],
            device_id={"height": 2 * y_dev[d] + c},
            device_id_type=MESH,
        )

    def o_copy(j):
        return pltpu.make_async_remote_copy(
            src_ref=oh.at[j, other],
            dst_ref=out.at[2 * j + c],
            send_sem=o_s.at[j],
            recv_sem=o_r.at[j],
            device_id=partner,
            device_id_type=MESH,
        )

    def o_store(j):
        return pltpu.make_async_copy(oh.at[j, c], out.at[2 * j + c], o_l.at[j])

    def z_count(g):
        return (nf + 1 - g) // 2

    def y_range(g):
        return (h0 + 1 - g) // 2, (h1 + 1 - g) // 2

    def send_z():
        top = (nf + 1) // 2
        for d in range(2):

            @pl.when(z_ok[d])
            def _():
                @pl.loop(0, top)
                def _(i):
                    j = top - 1 - i
                    for mine in (True, False):

                        @pl.when(j < z_count(c if mine else other))
                        def _():
                            z_copy(d, j, mine).start()

    send_z()

    @pl.loop(0, HALF)
    def _(j):
        own_copy(j).start()

    for d in range(2):

        @pl.when(y_ok[d])
        def _():
            for mine in (True, False):
                lo, hi = y_range(c if mine else other)

                @pl.loop(lo, hi)
                def _(j):
                    q_copy(d, j, mine).start()

    key_half = lax.broadcasted_iota(jnp.int32, (W, CHIP), 0) // TW
    query_half = lax.broadcasted_iota(jnp.int32, (W, CHIP), 1) % W // TW
    apart = jnp.where(key_half == query_half, 0.0, NEG).astype(jnp.float32)

    def width_bias(j):
        return apart * (1 - jnp.minimum(flags[2 * j + c, 2], 1)).astype(jnp.float32)

    def keys_of(block):
        return block[:, 0].reshape(CHIP, HD)

    def values_of(block):
        return jnp.concatenate([block[0, 1], block[1, 1]], axis=1)

    def queries_of(j, part):
        block = own[j, :, 2] if part == 0 else qn[part - 1, j]
        return block.reshape(CHIP, HD)

    def masked_scores(k, q, bias):
        s = dot(k, q, ((1,), (1,)))
        return (s.reshape(CHIP // W, W, CHIP) + bias[None]).reshape(CHIP, CHIP)

    def first(j, part, k, vt, bias):
        s = masked_scores(k, queries_of(j, part), bias)
        m = jnp.max(s, axis=0, keepdims=True)
        p = jnp.exp2((s - m) * SCALE)
        ml[j, part, 0:1] = m
        ml[j, part, 1:2] = jnp.sum(p, axis=0, keepdims=True)
        acc[j, part] = dot(vt, p.astype(jnp.bfloat16), ((1,), (0,)))

    def more(j, part, k, vt, bias):
        s = masked_scores(k, queries_of(j, part), bias)
        m_old = ml[j, part, 0:1]
        m = jnp.maximum(m_old, jnp.max(s, axis=0, keepdims=True))
        p = jnp.exp2((s - m) * SCALE)
        fade = jnp.exp2((m_old - m) * SCALE)
        ml[j, part, 0:1] = m
        ml[j, part, 1:2] = ml[j, part, 1:2] * fade + jnp.sum(p, axis=0, keepdims=True)
        acc[j, part] = acc[j, part] * fade + dot(vt, p.astype(jnp.bfloat16), ((1,), (0,)))

    def give_back(j):
        for d in range(2):
            m = ml[j, d + 1, 0:1]
            total = ml[j, d + 1, 1:2]
            rs[d, j, 0:HD] = (acc[j, d + 1] * (1.0 / total)).astype(jnp.bfloat16)
            level = m * SCALE + jnp.log2(total)
            a = level.astype(jnp.bfloat16).astype(jnp.float32)
            b = (level - a).astype(jnp.bfloat16).astype(jnp.float32)
            row = lax.broadcasted_iota(jnp.int32, (16, CHIP), 0)
            parts = jnp.where(row == 0, a, jnp.where(row == 1, b, jnp.where(row == 2, level - a - b, 0.0)))
            rs[d, j, HD : HD + 16] = parts.astype(jnp.bfloat16)

            @pl.when(y_ok[d])
            def _():
                ret_copy(d, j).start()

    def in_y(j):
        lo, hi = y_range(c)
        return (j >= lo) & (j < hi)

    def when_y(j, body):
        if h0 == 0 and h1 == HEADS:
            body()
        elif h0 < h1:
            pl.when(in_y(j))(body)

    my_z = z_count(c)

    @pl.loop(0, HALF)
    def _(i):
        j = HALF - 1 - i
        own_load(j).wait()
        own_copy(j).wait_recv()
        bias = width_bias(j)
        k, vt = keys_of(own[j]), values_of(own[j])

        def around():
            for d in range(2):

                @pl.when(y_ok[d])
                def _():
                    for half in range(2):
                        pltpu.make_async_remote_copy(
                            src_ref=qn.at[d, j, half],
                            dst_ref=qn.at[d, j, half],
                            send_sem=q_s.at[d, j, 0],
                            recv_sem=q_r.at[d, j, half],
                            device_id=partner,
                            device_id_type=MESH,
                        ).wait_recv()

            first(j, 1, k, vt, bias)
            first(j, 2, k, vt, bias)

            @pl.when(j >= my_z)
            def _():
                give_back(j)

        first(j, 0, k, vt, bias)
        when_y(j, around)

    @pl.loop(0, my_z)
    def _(i):
        j = my_z - 1 - i
        bias = width_bias(j) + (1 - jnp.minimum(flags[2 * j + c, 0], 1)).astype(jnp.float32) * NEG
        for d in range(2):

            @pl.when(z_ok[d])
            def _():
                for half in range(2):
                    pltpu.make_async_remote_copy(
                        src_ref=nb.at[d, j, half],
                        dst_ref=nb.at[d, j, half],
                        send_sem=z_s.at[d, j, 0],
                        recv_sem=z_r.at[d, j, half],
                        device_id=partner,
                        device_id_type=MESH,
                    ).wait_recv()
                k, vt = keys_of(nb[d, j]), values_of(nb[d, j])
                more(j, 0, k, vt, bias)

                def around():
                    more(j, 1, k, vt, bias)
                    more(j, 2, k, vt, bias)

                when_y(j, around)

        when_y(j, lambda: give_back(j))

    @pl.loop(0, HALF)
    def _(i):
        j = HALF - 1 - i
        low = (1 - jnp.minimum(flags[2 * j + c, 1], 1)).astype(jnp.float32) * NEG
        m = ml[j, 0, 0:1] * SCALE
        total = ml[j, 0, 1:2]

        def finish(o):
            o = o.T.astype(jnp.bfloat16)
            oh[j, 0] = o[:TOK]
            oh[j, 1] = o[TOK:]
            o_copy(j).start()
            o_store(j).start()

        def join():
            top = m + jnp.log2(total)
            levels = []
            for d in range(2):

                @pl.when(y_ok[d])
                def _():
                    ret_copy(1 - d, j).wait_recv()

                level = jnp.sum(rr[d, j, HD : HD + 16].astype(jnp.float32), axis=0, keepdims=True)
                levels.append(level + low + jnp.where(y_ok[d], 0.0, NEG))
            best = jnp.maximum(top, jnp.maximum(levels[0], levels[1]))
            w = jnp.exp2(m - best)
            num = acc[j, 0] * w
            den = total * w
            for d in range(2):
                w = jnp.exp2(levels[d] - best)
                num = num + rr[d, j, 0:HD].astype(jnp.float32) * w
                den = den + w
            finish(num * (1.0 / den))

        def alone():
            finish(acc[j, 0] * (1.0 / total))

        if h0 == 0 and h1 == HEADS:
            join()
        elif h0 == h1:
            alone()
        else:
            pl.when(in_y(j))(join)
            pl.when(jnp.logical_not(in_y(j)))(alone)

    @pl.loop(0, HALF)
    def _(j):
        own_copy(j).wait_send()
        o_copy(j).wait_send()
        o_store(j).wait()
        pltpu.make_async_remote_copy(
            src_ref=out.at[2 * j + other],
            dst_ref=out.at[2 * j + other],
            send_sem=o_s.at[j],
            recv_sem=o_r.at[j],
            device_id=partner,
            device_id_type=MESH,
        ).wait_recv()

    for d in range(2):
        for mine in (True, False):

            @pl.when(z_ok[d])
            def _():
                @pl.loop(0, z_count(c if mine else other))
                def _(j):
                    z_copy(d, j, mine).wait_send()

            @pl.when(y_ok[d])
            def _():
                lo, hi = y_range(c if mine else other)

                @pl.loop(lo, hi)
                def _(j):
                    q_copy(d, j, mine).wait_send()
                    if mine:
                        ret_copy(d, j).wait_send()


def attend(index, n_frame, n_chip_y, packed, flags):
    bf16, f32 = jnp.bfloat16, jnp.float32
    dma = pltpu.SemaphoreType.DMA
    return pl.pallas_call(
        functools.partial(kernel, PLANS[index], n_frame, n_chip_y),
        out_shape=jax.ShapeDtypeStruct((HEADS, TOK, HD), bf16),
        in_specs=[pl.BlockSpec(memory_space=pl.ANY), pl.BlockSpec(memory_space=pltpu.SMEM)],
        out_specs=pl.BlockSpec(memory_space=pl.ANY),
        scratch_shapes=[
            pltpu.VMEM((HALF, 2, 3, TOK, HD), bf16),
            pltpu.VMEM((2, HALF, 2, 2, TOK, HD), bf16),
            pltpu.VMEM((2, HALF, 2, TOK, HD), bf16),
            pltpu.VMEM((HALF, 3, HD, CHIP), f32),
            pltpu.VMEM((HALF, 3, 8, CHIP), f32),
            pltpu.VMEM((2, HALF, HD + 16, CHIP), bf16),
            pltpu.VMEM((2, HALF, HD + 16, CHIP), bf16),
            pltpu.VMEM((HALF, 2, TOK, HD), bf16),
            dma((HALF,)),
            dma((HALF,)),
            dma((HALF,)),
            dma((2, HALF, 2)),
            dma((2, HALF, 2)),
            dma((2, HALF, 2)),
            dma((2, HALF, 2)),
            dma((2, HALF)),
            dma((2, HALF)),
            dma((HALF,)),
            dma((HALF,)),
            dma((HALF,)),
        ],
        compiler_params=pltpu.CompilerParams(
            collective_id=index,
            has_side_effects=True,
            vmem_limit_bytes=32 * 1024 * 1024,
        ),
    )(packed, flags)


def shards(queries, key_value, windows):
    n_frame = lax.axis_size("frame")
    n_chip_y = lax.axis_size("height") // 2
    width = HEADS * HD
    vmem = pl.BlockSpec(memory_space=pltpu.VMEM)
    smem = pl.BlockSpec(memory_space=pltpu.SMEM)
    packed, flags, choice = pl.pallas_call(
        sort_kernel,
        out_shape=(
            jax.ShapeDtypeStruct((HEADS, 3, TOK, HD), jnp.bfloat16),
            jax.ShapeDtypeStruct((HEADS, 4), jnp.int32),
            jax.ShapeDtypeStruct((1,), jnp.int32),
        ),
        in_specs=[vmem, vmem, smem],
        out_specs=(vmem, smem, smem),
    )(queries.reshape(TOK, width), key_value.reshape(2, TOK, width), windows)
    branches = [functools.partial(attend, i, n_frame, n_chip_y) for i in range(len(PLANS))]
    slots = lax.switch(choice[0], branches, packed, flags)
    result = pl.pallas_call(
        place_kernel,
        out_shape=jax.ShapeDtypeStruct((TOK, width), jnp.bfloat16),
        in_specs=[vmem, smem],
        out_specs=vmem,
    )(slots, flags)
    return result.reshape(queries.shape)


def solution(mesh):
    in_specs = (
        P(("cand", "frame"), "height", None, None),
        P(None, ("cand", "frame"), "height", None, None),
        P(),
    )
    out_specs = P(("cand", "frame"), "height", None, None)
    return jax.shard_map(shards, mesh=mesh, in_specs=in_specs, out_specs=out_specs, check_vma=False)
```

```python
import functools
import math

import jax
import jax.numpy as jnp
from jax import lax
from jax.experimental import pallas as pl
from jax.experimental.pallas import tpu as pltpu
from jax.sharding import PartitionSpec as P

HEADS = 12
HALF = HEADS // 2
HD = 128
TOK = 128
CHIP = 2 * TOK
W = 16
TW = 8
NEG = -1e30
EXTRA = 16
SCALE = math.log2(math.e) / math.sqrt(HD)
MESH = pl.DeviceIdType.MESH


def dot(a, b, dims):
    return lax.dot_general(a, b, ((dims[0], dims[1]), ((), ())), preferred_element_type=jnp.float32)


PLANS = (
    (4, 0, 8),
    (5, 2, 10),
    (5, 0, 10),
    (6, 2, 10),
    (7, 2, 10),
    (8, 4, 12),
    (7, 0, 12),
    (9, 2, 12),
    (12, 0, 12),
)


def sort_kernel(q, kv, win, packed, flags, choice):
    keys, tall, wide, lone = [], jnp.int32(0), jnp.int32(0), jnp.int32(0)
    for h in range(HEADS):
        wf, wh = jnp.minimum(win[0, h], 1), jnp.minimum(win[1, h], 1)
        keys.append((3 - 3 * wf - wh + 2 * wf * wh) * 16 + h)
        wide = wide + wf
        tall = tall + wh
        lone = lone + wf * (1 - wh)
    ranks = []
    for h in range(HEADS):
        rank = jnp.int32(0)
        for k in range(HEADS):
            if k != h:
                rank = rank + jnp.where(keys[k] < keys[h], 1, 0)
        ranks.append(rank)
    for s in range(HEADS):
        head = jnp.int32(0)
        for h in range(HEADS):
            head = head + jnp.where(ranks[h] == s, h, 0)
        for i in range(3):
            flags[s, i] = win[i, head]
        flags[s, 3] = ranks[s]
        col = pl.multiple_of(head * HD, HD)
        g, j = s % 2, s // 2
        packed[g, j, 0] = kv[0, :, pl.ds(col, HD)]
        packed[g, j, 1] = kv[1, :, pl.ds(col, HD)].T
        packed[g, j, 2] = q[:, pl.ds(col, HD)]
    best = jnp.int32(len(PLANS) - 1)
    for i in reversed(range(len(PLANS) - 1)):
        nf, h0, h1 = PLANS[i]
        best = jnp.where((wide <= nf) & (lone >= h0) & (lone + tall <= h1), i, best)
    choice[0] = best


def place_kernel(o, flags, out):
    for h in range(HEADS):
        out[:, h * HD : (h + 1) * HD] = o[flags[h, 3]]


def kernel(
    cfg,
    n_frame,
    n_chip_y,
    packed,
    flags,
    out,
    kv,
    qa,
    acc,
    top,
    rs,
    rr,
    oh,
    own_l,
    own_s,
    own_r,
    z_s,
    z_r,
    q_s,
    q_r,
    ret_s,
    ret_r,
    o_l,
    o_s,
    o_r,
):
    nf, h0, h1 = cfg
    lo, hi = h0 // 2, h1 // 2
    halves = ((HALF // 2, HALF), (0, HALF // 2))
    runs = tuple((max(a, lo), min(b, hi)) for a, b in halves)
    f = lax.axis_index("frame")
    height = lax.axis_index("height")
    y = height // 2
    c = height % 2
    other = 1 - c
    z_ok = (f > 0, f < n_frame - 1)
    y_ok = (y > 0, y < n_chip_y - 1)
    z_dev = (f - 1, f + 1)
    y_dev = (y - 1, y + 1)
    partner = {"height": 2 * y + other}

    barrier = pltpu.get_barrier_semaphore()
    pl.semaphore_signal(barrier, inc=1, device_id=partner, device_id_type=MESH)
    for d in range(2):

        @pl.when(z_ok[d])
        def _():
            for g in range(2):
                pl.semaphore_signal(
                    barrier,
                    inc=1,
                    device_id={"frame": z_dev[d], "height": 2 * y + g},
                    device_id_type=MESH,
                )

        @pl.when(y_ok[d])
        def _():
            for g in range(2):
                pl.semaphore_signal(
                    barrier,
                    inc=1,
                    device_id={"height": 2 * y_dev[d] + g},
                    device_id_type=MESH,
                )

    def own_loads(i):
        j, n = halves[i][0], halves[i][1] - halves[i][0]
        return (
            pltpu.make_async_copy(
                packed.at[c, pl.ds(j, n), pl.ds(0, 2)], kv.at[1, pl.ds(j, n), c], own_l.at[i, 0]
            ),
            pltpu.make_async_copy(
                packed.at[c, pl.ds(j, n), 2], qa.at[pl.ds(j, n), 0, c], own_l.at[i, 1]
            ),
        )

    def remote(src, dst, send_sem, recv_sem, device):
        return pltpu.make_async_remote_copy(
            src_ref=src,
            dst_ref=dst,
            send_sem=send_sem,
            recv_sem=recv_sem,
            device_id=device,
            device_id_type=MESH,
        )

    def own_copies(i):
        j, n = halves[i][0], halves[i][1] - halves[i][0]
        return (
            remote(
                packed.at[other, pl.ds(j, n), pl.ds(0, 2)],
                kv.at[1, pl.ds(j, n), c],
                own_s.at[i, 0],
                own_r.at[i, 0],
                partner,
            ),
            remote(
                packed.at[other, pl.ds(j, n), 2],
                qa.at[pl.ds(j, n), 0, c],
                own_s.at[i, 1],
                own_r.at[i, 1],
                partner,
            ),
        )

    def z_copy(d, j, g):
        return remote(
            packed.at[g, j, pl.ds(0, 2)],
            kv.at[2 - 2 * d, j, c],
            z_s.at[d, j, g],
            z_r.at[1 - d, j, c],
            {"frame": z_dev[d], "height": 2 * y + g},
        )

    def z_arrival(d, j, half):
        dst = kv.at[2 * d, j, half]
        return remote(dst, dst, z_s.at[d, j, 0], z_r.at[d, j, half], partner)

    def q_copy(d, i, g):
        j, n = runs[i][0], runs[i][1] - runs[i][0]
        return remote(
            packed.at[g, pl.ds(j, n), 2],
            qa.at[pl.ds(j, n), 2 - d, c],
            q_s.at[d, i, g],
            q_r.at[1 - d, i, c],
            {"height": 2 * y_dev[d] + g},
        )

    def q_arrival(d, i, half):
        j, n = runs[i][0], runs[i][1] - runs[i][0]
        dst = qa.at[pl.ds(j, n), 1 + d, half]
        return remote(dst, dst, q_s.at[d, i, 0], q_r.at[d, i, half], partner)

    def ret_copy(d, j):
        return remote(
            rs.at[d, j],
            rr.at[1 - d, j],
            ret_s.at[d, j],
            ret_r.at[1 - d, j],
            {"height": 2 * y_dev[d] + c},
        )

    def o_copy(j):
        return remote(oh.at[j, other], out.at[2 * j + c], o_s.at[j], o_r.at[j], partner)

    def o_arrival(j):
        dst = out.at[2 * j + other]
        return remote(dst, dst, o_s.at[j], o_r.at[j], partner)

    def o_store(j):
        return pltpu.make_async_copy(oh.at[j, c], out.at[2 * j + c], o_l.at[j])

    for i in range(2):
        for copy in own_loads(i):
            copy.start()

    for d in range(2):

        @pl.when(jnp.logical_not(y_ok[d]))
        def _():
            rr[d] = jnp.zeros(rr.shape[1:], rr.dtype)

        @pl.when(jnp.logical_not(z_ok[d]))
        def _():
            kv[2 * d] = jnp.zeros(kv.shape[1:], kv.dtype)

    pl.semaphore_wait(
        barrier,
        1
        + 2 * sum(jnp.where(ok, 1, 0) for ok in z_ok)
        + 2 * sum(jnp.where(ok, 1, 0) for ok in y_ok),
    )

    for copy in own_copies(0):
        copy.start()
    for d in range(2):

        @pl.when(z_ok[d])
        def _():
            for s in reversed(range(nf)):
                z_copy(d, s // 2, s % 2).start()

    for copy in own_copies(1):
        copy.start()
    for i in range(2):
        for d in range(2):

            @pl.when(y_ok[d])
            def _():
                for g in range(2):
                    q_copy(d, i, g).start()

    key_side = lax.broadcasted_iota(jnp.int32, (W, CHIP), 0) // TW
    query_side = lax.broadcasted_iota(jnp.int32, (W, CHIP), 1) % W // TW
    apart = jnp.where(key_side == query_side, 0.0, NEG).astype(jnp.float32)
    ones = jnp.ones((EXTRA, CHIP), jnp.bfloat16)

    def shut(j, column):
        return (1 - flags[2 * j + c, column]).astype(jnp.float32)

    def scores(tile, j, part, bias):
        k = kv[tile, j, :, 0].reshape(CHIP, HD)
        s = dot(k, qa[j, part].reshape(CHIP, HD), ((1,), (1,)))
        return (s.reshape(CHIP // W, W, CHIP) + bias[None]).reshape(CHIP, CHIP)

    def values(tile, j):
        vt = jnp.concatenate([kv[tile, j, 0, 1], kv[tile, j, 1, 1]], axis=1)
        return jnp.concatenate([vt, ones], axis=0)

    def weights(s, m):
        return jnp.exp2((s - m) * SCALE).astype(jnp.bfloat16)

    def here(j, parts):
        bias = apart * shut(j, 2)
        vt = values(1, j)
        found = [scores(1, j, part, bias) for part in parts]
        tops = [jnp.max(s, axis=0, keepdims=True) for s in found]
        sums = [dot(vt, weights(s, m), ((1,), (0,))) for s, m in zip(found, tops)]
        for part, m, o in zip(parts, tops, sums):
            top[j, part, 0:1] = m
            acc[j, part] = o

    def around(j, parts):
        width = apart * shut(j, 2)
        closed = shut(j, 0) * NEG
        bias = [width + jnp.where(z_ok[d], closed, NEG) for d in range(2)]
        vt = jnp.concatenate([values(0, j), values(2, j)], axis=1)
        found = [[scores(2 * d, j, part, bias[d]) for d in range(2)] for part in parts]
        old = [top[j, part, 0:1] for part in parts]
        before = [acc[j, part] for part in parts]
        results = []
        for pair, m_old, o_old in zip(found, old, before):
            m = jnp.maximum(pair[0], pair[1])
            m = jnp.maximum(m_old, jnp.max(m, axis=0, keepdims=True))
            p = jnp.concatenate([weights(s, m) for s in pair], axis=0)
            o = o_old * jnp.exp2((m_old - m) * SCALE) + dot(vt, p, ((1,), (0,)))
            results.append((m, o))
        for part, (m, o) in zip(parts, results):
            top[j, part, 0:1] = m
            acc[j, part] = o

    def give_back(j):
        for d in range(2):
            m = top[j, d + 1, 0:1]
            total = acc[j, d + 1, HD : HD + 1]
            rs[d, j, 0:HD] = (acc[j, d + 1, 0:HD] * (1.0 / total)).astype(jnp.bfloat16)
            level = m * SCALE + jnp.log2(total)
            a = level.astype(jnp.bfloat16).astype(jnp.float32)
            b = (level - a).astype(jnp.bfloat16).astype(jnp.float32)
            row = lax.broadcasted_iota(jnp.int32, (EXTRA, CHIP), 0)
            rest = jnp.where(row == 2, level - a - b, 0.0)
            digits = jnp.where(row == 0, a, jnp.where(row == 1, b, rest))
            rs[d, j, HD : HD + EXTRA] = digits.astype(jnp.bfloat16)
        for d in range(2):

            @pl.when(y_ok[d])
            def _():
                ret_copy(d, j).start()

    def finish(j, o):
        o = o.T.astype(jnp.bfloat16)
        oh[j, 0] = o[:TOK]
        oh[j, 1] = o[TOK:]
        o_copy(j).start()
        o_store(j).start()

    def alone(j):
        finish(j, acc[j, 0, 0:HD] * (1.0 / acc[j, 0, HD : HD + 1]))

    def join(j):
        for d in range(2):

            @pl.when(y_ok[d])
            def _():
                ret_copy(1 - d, j).wait_recv()

        m = top[j, 0, 0:1] * SCALE
        total = acc[j, 0, HD : HD + 1]
        low = shut(j, 1) * NEG
        levels = []
        for d in range(2):
            level = jnp.sum(rr[d, j, HD : HD + EXTRA].astype(jnp.float32), axis=0, keepdims=True)
            levels.append(level + jnp.where(y_ok[d], low, NEG))
        best = jnp.maximum(m + jnp.log2(total), jnp.maximum(levels[0], levels[1]))
        w = [jnp.exp2(x - best) for x in (m, *levels)]
        over = 1.0 / (total * w[0] + w[1] + w[2])
        o = acc[j, 0, 0:HD] * (w[0] * over)
        for d in range(2):
            o = o + rr[d, j, 0:HD].astype(jnp.float32) * (w[d + 1] * over)
        finish(j, o)

    my_z = (nf + 1 - c) // 2
    both = (0, 1, 2)

    for i in range(2):
        for copy in own_loads(i):
            copy.wait()
        for copy in own_copies(i):
            copy.wait_recv()
        first, last = runs[i]
        for a, b in ((halves[i][0], first), (last, halves[i][1])):
            for j in range(a, b):
                here(j, (0,))

    for i in range(2):
        first, last = runs[i]
        for d in range(2):

            @pl.when(y_ok[d])
            def _():
                for half in range(2):
                    q_arrival(d, i, half).wait_recv()

        @pl.loop(0, last - first)
        def _(n):
            j = last - 1 - n
            here(j, both)

            @pl.when(j >= my_z)
            def _():
                give_back(j)

    @pl.loop(jnp.maximum(my_z, hi), HALF)
    def _(j):
        alone(j)

    @pl.loop(0, hi - jnp.maximum(my_z, lo))
    def _(n):
        join(hi - 1 - n)

    def wait_z(j):
        for d in range(2):

            @pl.when(z_ok[d])
            def _():
                for half in range(2):
                    z_arrival(d, j, half).wait_recv()

    @pl.loop(0, my_z - lo)
    def _(n):
        j = my_z - 1 - n
        wait_z(j)
        around(j, both)
        give_back(j)

    for j in reversed(range(lo)):
        wait_z(j)
        around(j, (0,))
        alone(j)

    @pl.loop(0, my_z - lo)
    def _(n):
        join(my_z - 1 - n)

    for i in range(2):
        for copy in own_copies(i):
            copy.wait_send()
    for d in range(2):

        @pl.when(z_ok[d])
        def _():
            for s in range(nf):
                z_copy(d, s // 2, s % 2).wait_send()

        @pl.when(y_ok[d])
        def _():
            for i in range(2):
                for g in range(2):
                    q_copy(d, i, g).wait_send()

            @pl.loop(lo, hi)
            def _(j):
                ret_copy(d, j).wait_send()

    @pl.loop(0, HALF)
    def _(j):
        o_store(j).wait()
        o_copy(j).wait_send()
        o_arrival(j).wait_recv()


def attend(index, n_frame, n_chip_y, packed, flags):
    nf, h0, h1 = PLANS[index]
    assert h0 % 2 == 0 and h1 % 2 == 0 and h0 <= min(nf, HALF - 2) and max(nf, HALF + 2) <= h1
    bf16, f32 = jnp.bfloat16, jnp.float32
    dma = pltpu.SemaphoreType.DMA
    return pl.pallas_call(
        functools.partial(kernel, PLANS[index], n_frame, n_chip_y),
        out_shape=jax.ShapeDtypeStruct((HEADS, TOK, HD), bf16),
        in_specs=[pl.BlockSpec(memory_space=pl.ANY), pl.BlockSpec(memory_space=pltpu.SMEM)],
        out_specs=pl.BlockSpec(memory_space=pl.ANY),
        scratch_shapes=[
            pltpu.VMEM((3, HALF, 2, 2, TOK, HD), bf16),
            pltpu.VMEM((HALF, 3, 2, TOK, HD), bf16),
            pltpu.VMEM((HALF, 3, HD + EXTRA, CHIP), f32),
            pltpu.VMEM((HALF, 3, 8, CHIP), f32),
            pltpu.VMEM((2, HALF, HD + EXTRA, CHIP), bf16),
            pltpu.VMEM((2, HALF, HD + EXTRA, CHIP), bf16),
            pltpu.VMEM((HALF, 2, TOK, HD), bf16),
            dma((2, 2)),
            dma((2, 2)),
            dma((2, 2)),
            dma((2, HALF, 2)),
            dma((2, HALF, 2)),
            dma((2, 2, 2)),
            dma((2, 2, 2)),
            dma((2, HALF)),
            dma((2, HALF)),
            dma((HALF,)),
            dma((HALF,)),
            dma((HALF,)),
        ],
        compiler_params=pltpu.CompilerParams(
            collective_id=index,
            has_side_effects=True,
            vmem_limit_bytes=32 * 1024 * 1024,
        ),
    )(packed, flags)


def shards(queries, key_value, windows):
    n_frame = lax.axis_size("frame")
    n_chip_y = lax.axis_size("height") // 2
    width = HEADS * HD
    vmem = pl.BlockSpec(memory_space=pltpu.VMEM)
    smem = pl.BlockSpec(memory_space=pltpu.SMEM)
    packed, flags, choice = pl.pallas_call(
        sort_kernel,
        out_shape=(
            jax.ShapeDtypeStruct((2, HALF, 3, TOK, HD), jnp.bfloat16),
            jax.ShapeDtypeStruct((HEADS, 4), jnp.int32),
            jax.ShapeDtypeStruct((1,), jnp.int32),
        ),
        in_specs=[vmem, vmem, smem],
        out_specs=(vmem, smem, smem),
    )(queries.reshape(TOK, width), key_value.reshape(2, TOK, width), windows.T)
    branches = [functools.partial(attend, i, n_frame, n_chip_y) for i in range(len(PLANS))]
    slots = lax.switch(choice[0], branches, packed, flags)
    result = pl.pallas_call(
        place_kernel,
        out_shape=jax.ShapeDtypeStruct((TOK, width), jnp.bfloat16),
        in_specs=[vmem, smem],
        out_specs=vmem,
    )(slots, flags)
    return result.reshape(queries.shape)


def solution(mesh):
    in_specs = (
        P(("cand", "frame"), "height", None, None),
        P(None, ("cand", "frame"), "height", None, None),
        P(),
    )
    out_specs = P(("cand", "frame"), "height", None, None)
    return jax.shard_map(shards, mesh=mesh, in_specs=in_specs, out_specs=out_specs, check_vma=False)
```

```python
import functools
import math

import jax
import jax.numpy as jnp
from jax import lax
from jax.experimental import pallas as pl
from jax.experimental.pallas import tpu as pltpu
from jax.sharding import PartitionSpec as P

HEADS = 12
HALF = HEADS // 2
HD = 128
TOK = 128
CHIP = 2 * TOK
W = 16
TW = 8
NEG = -1e30
EXTRA = 16
SCALE = math.log2(math.e) / math.sqrt(HD)
MESH = pl.DeviceIdType.MESH


def dot(a, b, dims):
    return lax.dot_general(a, b, ((dims[0], dims[1]), ((), ())), preferred_element_type=jnp.float32)


PLANS = (
    (4, 2, 10),
    (4, 0, 8),
    (5, 2, 10),
    (6, 2, 10),
    (5, 0, 10),
    (7, 2, 12),
    (8, 2, 12),
    (7, 0, 12),
    (9, 2, 12),
    (12, 0, 12),
)


def sort_kernel(q, kv, win, packed, flags, choice, kvin, qin, order, sem):
    loads = (
        pltpu.make_async_copy(kv.at[0], kvin.at[0], sem.at[0]),
        pltpu.make_async_copy(kv.at[1], kvin.at[1], sem.at[1]),
        pltpu.make_async_copy(q, qin, sem.at[2]),
    )
    for load in loads:
        load.start()
    wf = [win[0, h] for h in range(HEADS)]
    wh = [win[1, h] for h in range(HEADS)]
    kinds = [(a - a * b, a * b, b - a * b, (1 - a) * (1 - b)) for a, b in zip(wf, wh)]
    count = [sum(kind[i] for kind in kinds) for i in range(4)]
    free = [jnp.int32(0), count[0], count[0] + count[1], count[0] + count[1] + count[2]]
    for h, kind in enumerate(kinds):
        rank = sum(x * place for x, place in zip(kind, free))
        free = [place + x for x, place in zip(kind, free)]
        order[rank] = jnp.int32(h)
        for i in range(3):
            flags[rank, i] = win[i, h]
        flags[h, 3] = rank
    wide, lone, tall = count[0] + count[1], count[0], count[1] + count[2]
    best = jnp.int32(len(PLANS) - 1)
    for i in reversed(range(len(PLANS) - 1)):
        nf, h0, h1 = PLANS[i]
        best = jnp.where((wide <= nf) & (lone >= h0) & (lone + tall <= h1), i, best)
    choice[0] = best
    for kind in range(3):
        loads[kind].wait()
        for s in range(HEADS):
            columns = pl.ds(pl.multiple_of(order[s] * HD, HD), HD)
            block = qin[:, columns] if kind == 2 else kvin[kind, :, columns]
            packed[s % 2, s // 2, kind] = block.T if kind == 1 else block


def place_kernel(o, flags, out):
    for h in range(HEADS):
        out[:, h * HD : (h + 1) * HD] = o[flags[h, 3]]


def kernel(
    cfg,
    n_frame,
    n_chip_y,
    packed,
    flags,
    out,
    kv,
    qa,
    acc,
    top,
    rs,
    rr,
    oh,
    own_l,
    own_s,
    own_r,
    z_s,
    z_r,
    q_s,
    q_r,
    ret_s,
    ret_r,
    o_l,
    o_s,
    o_r,
):
    nf, h0, h1 = cfg
    lo, hi = h0 // 2, h1 // 2
    halves = ((HALF // 2, HALF), (0, HALF // 2))
    runs = tuple((max(a, lo), min(b, hi)) for a, b in halves)
    f = lax.axis_index("frame")
    height = lax.axis_index("height")
    y = height // 2
    c = height % 2
    other = 1 - c
    z_ok = (f > 0, f < n_frame - 1)
    y_ok = (y > 0, y < n_chip_y - 1)
    z_dev = (f - 1, f + 1)
    y_dev = (y - 1, y + 1)
    partner = {"height": 2 * y + other}

    barrier = pltpu.get_barrier_semaphore()
    pl.semaphore_signal(barrier, inc=1, device_id=partner, device_id_type=MESH)
    for d in range(2):

        @pl.when(z_ok[d])
        def _():
            for g in range(2):
                pl.semaphore_signal(
                    barrier,
                    inc=1,
                    device_id={"frame": z_dev[d], "height": 2 * y + g},
                    device_id_type=MESH,
                )

        @pl.when(y_ok[d])
        def _():
            for g in range(2):
                pl.semaphore_signal(
                    barrier,
                    inc=1,
                    device_id={"height": 2 * y_dev[d] + g},
                    device_id_type=MESH,
                )

    def own_loads(i):
        j, n = halves[i][0], halves[i][1] - halves[i][0]
        return (
            pltpu.make_async_copy(
                packed.at[c, pl.ds(j, n), pl.ds(0, 2)], kv.at[1, pl.ds(j, n), c], own_l.at[i, 0]
            ),
            pltpu.make_async_copy(
                packed.at[c, pl.ds(j, n), 2], qa.at[pl.ds(j, n), 0, c], own_l.at[i, 1]
            ),
        )

    def remote(src, dst, send_sem, recv_sem, device):
        return pltpu.make_async_remote_copy(
            src_ref=src,
            dst_ref=dst,
            send_sem=send_sem,
            recv_sem=recv_sem,
            device_id=device,
            device_id_type=MESH,
        )

    def own_copies(i):
        j, n = halves[i][0], halves[i][1] - halves[i][0]
        return (
            remote(
                packed.at[other, pl.ds(j, n), pl.ds(0, 2)],
                kv.at[1, pl.ds(j, n), c],
                own_s.at[i, 0],
                own_r.at[i, 0],
                partner,
            ),
            remote(
                packed.at[other, pl.ds(j, n), 2],
                qa.at[pl.ds(j, n), 0, c],
                own_s.at[i, 1],
                own_r.at[i, 1],
                partner,
            ),
        )

    def z_copy(d, j, g):
        return remote(
            packed.at[g, j, pl.ds(0, 2)],
            kv.at[2 - 2 * d, j, c],
            z_s.at[d, j, g],
            z_r.at[1 - d, j, c],
            {"frame": z_dev[d], "height": 2 * y + g},
        )

    def z_arrival(d, j, half):
        dst = kv.at[2 * d, j, half]
        return remote(dst, dst, z_s.at[d, j, 0], z_r.at[d, j, half], partner)

    def q_copy(d, i, g):
        j, n = runs[i][0], runs[i][1] - runs[i][0]
        return remote(
            packed.at[g, pl.ds(j, n), 2],
            qa.at[pl.ds(j, n), 2 - d, c],
            q_s.at[d, i, g],
            q_r.at[1 - d, i, c],
            {"height": 2 * y_dev[d] + g},
        )

    def q_arrival(d, i, half):
        j, n = runs[i][0], runs[i][1] - runs[i][0]
        dst = qa.at[pl.ds(j, n), 1 + d, half]
        return remote(dst, dst, q_s.at[d, i, 0], q_r.at[d, i, half], partner)

    def ret_copy(d, j):
        return remote(
            rs.at[d, j],
            rr.at[1 - d, j],
            ret_s.at[d, j],
            ret_r.at[1 - d, j],
            {"height": 2 * y_dev[d] + c},
        )

    def o_copy(j):
        return remote(oh.at[j, other], out.at[2 * j + c], o_s.at[j], o_r.at[j], partner)

    def o_arrival(j):
        dst = out.at[2 * j + other]
        return remote(dst, dst, o_s.at[j], o_r.at[j], partner)

    def o_store(j):
        return pltpu.make_async_copy(oh.at[j, c], out.at[2 * j + c], o_l.at[j])

    for i in range(2):
        for copy in own_loads(i):
            copy.start()

    for d in range(2):

        @pl.when(jnp.logical_not(y_ok[d]))
        def _():
            rr[d] = jnp.zeros(rr.shape[1:], rr.dtype)

        @pl.when(jnp.logical_not(z_ok[d]))
        def _():
            kv[2 * d] = jnp.zeros(kv.shape[1:], kv.dtype)

    pl.semaphore_wait(
        barrier,
        1
        + 2 * sum(jnp.where(ok, 1, 0) for ok in z_ok)
        + 2 * sum(jnp.where(ok, 1, 0) for ok in y_ok),
    )

    def send_z(slots):
        for d in range(2):

            @pl.when(z_ok[d])
            def _():
                for s in slots:
                    z_copy(d, s // 2, s % 2).start()

    z_order = tuple(reversed(range(nf)))
    for copy in own_copies(0):
        copy.start()
    send_z(z_order[:4])
    for copy in own_copies(1):
        copy.start()
    for i in range(2):
        for d in range(2):

            @pl.when(y_ok[d])
            def _():
                for g in range(2):
                    q_copy(d, i, g).start()

    key_side = lax.broadcasted_iota(jnp.int32, (W, CHIP), 0) // TW
    query_side = lax.broadcasted_iota(jnp.int32, (W, CHIP), 1) % W // TW
    apart = jnp.where(key_side == query_side, 0.0, NEG).astype(jnp.float32)
    ones = jnp.ones((EXTRA, CHIP), jnp.bfloat16)

    def shut(j, column):
        return (1 - flags[2 * j + c, column]).astype(jnp.float32)

    def scores(tile, j, part, bias):
        k = kv[tile, j, :, 0].reshape(CHIP, HD)
        s = dot(k, qa[j, part].reshape(CHIP, HD), ((1,), (1,)))
        return (s.reshape(CHIP // W, W, CHIP) + bias[None]).reshape(CHIP, CHIP)

    def values(tile, j):
        vt = jnp.concatenate([kv[tile, j, 0, 1], kv[tile, j, 1, 1]], axis=1)
        return jnp.concatenate([vt, ones], axis=0)

    def weights(s, m):
        return jnp.exp2((s - m) * SCALE).astype(jnp.bfloat16)

    def here(j, parts):
        bias = apart * shut(j, 2)
        vt = values(1, j)
        found = [scores(1, j, part, bias) for part in parts]
        tops = [jnp.max(s, axis=0, keepdims=True) for s in found]
        sums = [dot(vt, weights(s, m), ((1,), (0,))) for s, m in zip(found, tops)]
        for part, m, o in zip(parts, tops, sums):
            top[j, part, 0:1] = m
            acc[j, part] = o

    def around(j, parts):
        width = apart * shut(j, 2)
        closed = shut(j, 0) * NEG
        bias = [width + jnp.where(z_ok[d], closed, NEG) for d in range(2)]
        bias = jnp.stack(bias)[:, None]
        vt = jnp.concatenate([values(0, j), values(2, j)], axis=1)
        k = jnp.concatenate([kv[2 * d, j, :, 0].reshape(CHIP, HD) for d in range(2)], axis=0)
        found = []
        for part in parts:
            s = dot(k, qa[j, part].reshape(CHIP, HD), ((1,), (1,)))
            found.append((s.reshape(2, CHIP // W, W, CHIP) + bias).reshape(2 * CHIP, CHIP))
        old = [top[j, part, 0:1] for part in parts]
        before = [acc[j, part] for part in parts]
        results = []
        for s, m_old, o_old in zip(found, old, before):
            m = jnp.maximum(m_old, jnp.max(s, axis=0, keepdims=True))
            o = o_old * jnp.exp2((m_old - m) * SCALE) + dot(vt, weights(s, m), ((1,), (0,)))
            results.append((m, o))
        for part, (m, o) in zip(parts, results):
            top[j, part, 0:1] = m
            acc[j, part] = o

    def give_back(j):
        for d in range(2):
            m = top[j, d + 1, 0:1]
            total = acc[j, d + 1, HD : HD + 1]
            rs[d, j, 0:HD] = (acc[j, d + 1, 0:HD] * (1.0 / total)).astype(jnp.bfloat16)
            level = m * SCALE + jnp.log2(total)
            a = level.astype(jnp.bfloat16).astype(jnp.float32)
            b = (level - a).astype(jnp.bfloat16).astype(jnp.float32)
            row = lax.broadcasted_iota(jnp.int32, (EXTRA, CHIP), 0)
            rest = jnp.where(row == 2, level - a - b, 0.0)
            digits = jnp.where(row == 0, a, jnp.where(row == 1, b, rest))
            rs[d, j, HD : HD + EXTRA] = digits.astype(jnp.bfloat16)
        for d in range(2):

            @pl.when(y_ok[d])
            def _():
                ret_copy(d, j).start()

    def finish(j, o):
        o = o.T.astype(jnp.bfloat16)
        oh[j, 0] = o[:TOK]
        oh[j, 1] = o[TOK:]
        o_copy(j).start()
        o_store(j).start()

    def alone(j):
        finish(j, acc[j, 0, 0:HD] * (1.0 / acc[j, 0, HD : HD + 1]))

    def join(j):
        for d in range(2):

            @pl.when(y_ok[d])
            def _():
                ret_copy(1 - d, j).wait_recv()

        m = top[j, 0, 0:1] * SCALE
        total = acc[j, 0, HD : HD + 1]
        low = shut(j, 1) * NEG
        levels = []
        for d in range(2):
            level = jnp.sum(rr[d, j, HD : HD + EXTRA].astype(jnp.float32), axis=0, keepdims=True)
            levels.append(level + jnp.where(y_ok[d], low, NEG))
        best = jnp.maximum(m + jnp.log2(total), jnp.maximum(levels[0], levels[1]))
        w = [jnp.exp2(x - best) for x in (m, *levels)]
        over = 1.0 / (total * w[0] + w[1] + w[2])
        o = acc[j, 0, 0:HD] * (w[0] * over)
        for d in range(2):
            o = o + rr[d, j, 0:HD].astype(jnp.float32) * (w[d + 1] * over)
        finish(j, o)

    my_z = (nf + 1 - c) // 2
    both = (0, 1, 2)

    for i in range(2):
        for copy in own_loads(i):
            copy.wait()
        for copy in own_copies(i):
            copy.wait_recv()
        first, last = runs[i]
        for a, b in ((halves[i][0], first), (last, halves[i][1])):
            for j in range(a, b):
                here(j, (0,))

    send_z(z_order[4:])

    for i in range(2):
        first, last = runs[i]
        for d in range(2):

            @pl.when(y_ok[d])
            def _():
                for half in range(2):
                    q_arrival(d, i, half).wait_recv()

        @pl.loop(0, last - first)
        def _(n):
            j = last - 1 - n
            here(j, both)

            @pl.when(j >= my_z)
            def _():
                give_back(j)

    @pl.loop(jnp.maximum(my_z, hi), HALF)
    def _(j):
        alone(j)

    @pl.loop(0, hi - jnp.maximum(my_z, lo))
    def _(n):
        join(hi - 1 - n)

    for i in range(2):
        for copy in own_copies(i):
            copy.wait_send()
    for d in range(2):

        @pl.when(y_ok[d])
        def _():
            for i in range(2):
                for g in range(2):
                    q_copy(d, i, g).wait_send()

    def wait_z(j):
        for d in range(2):

            @pl.when(z_ok[d])
            def _():
                for half in range(2):
                    z_arrival(d, j, half).wait_recv()

    @pl.loop(0, my_z - lo)
    def _(n):
        j = my_z - 1 - n
        wait_z(j)
        around(j, both)
        give_back(j)

    for j in reversed(range(lo)):
        wait_z(j)
        around(j, (0,))
        alone(j)

    @pl.loop(0, my_z - lo)
    def _(n):
        join(my_z - 1 - n)

    for d in range(2):

        @pl.when(z_ok[d])
        def _():
            for s in range(nf):
                z_copy(d, s // 2, s % 2).wait_send()

        @pl.when(y_ok[d])
        def _():
            @pl.loop(lo, hi)
            def _(j):
                ret_copy(d, j).wait_send()

    @pl.loop(0, HALF)
    def _(j):
        o_store(j).wait()
        o_copy(j).wait_send()
        o_arrival(j).wait_recv()


def attend(index, n_frame, n_chip_y, packed, flags):
    nf, h0, h1 = PLANS[index]
    assert h0 % 2 == 0 and h1 % 2 == 0 and h0 <= min(nf, HALF - 2) and max(nf, HALF + 2) <= h1
    bf16, f32 = jnp.bfloat16, jnp.float32
    dma = pltpu.SemaphoreType.DMA
    return pl.pallas_call(
        functools.partial(kernel, PLANS[index], n_frame, n_chip_y),
        out_shape=jax.ShapeDtypeStruct((HEADS, TOK, HD), bf16),
        in_specs=[pl.BlockSpec(memory_space=pl.ANY), pl.BlockSpec(memory_space=pltpu.SMEM)],
        out_specs=pl.BlockSpec(memory_space=pl.ANY),
        scratch_shapes=[
            pltpu.VMEM((3, HALF, 2, 2, TOK, HD), bf16),
            pltpu.VMEM((HALF, 3, 2, TOK, HD), bf16),
            pltpu.VMEM((HALF, 3, HD + EXTRA, CHIP), f32),
            pltpu.VMEM((HALF, 3, 8, CHIP), f32),
            pltpu.VMEM((2, HALF, HD + EXTRA, CHIP), bf16),
            pltpu.VMEM((2, HALF, HD + EXTRA, CHIP), bf16),
            pltpu.VMEM((HALF, 2, TOK, HD), bf16),
            dma((2, 2)),
            dma((2, 2)),
            dma((2, 2)),
            dma((2, HALF, 2)),
            dma((2, HALF, 2)),
            dma((2, 2, 2)),
            dma((2, 2, 2)),
            dma((2, HALF)),
            dma((2, HALF)),
            dma((HALF,)),
            dma((HALF,)),
            dma((HALF,)),
        ],
        compiler_params=pltpu.CompilerParams(
            collective_id=index,
            has_side_effects=True,
            vmem_limit_bytes=32 * 1024 * 1024,
        ),
    )(packed, flags)


def shards(queries, key_value, windows):
    n_frame = lax.axis_size("frame")
    n_chip_y = lax.axis_size("height") // 2
    width = HEADS * HD
    vmem = pl.BlockSpec(memory_space=pltpu.VMEM)
    smem = pl.BlockSpec(memory_space=pltpu.SMEM)
    packed, flags, choice = pl.pallas_call(
        sort_kernel,
        out_shape=(
            jax.ShapeDtypeStruct((2, HALF, 3, TOK, HD), jnp.bfloat16),
            jax.ShapeDtypeStruct((HEADS, 4), jnp.int32),
            jax.ShapeDtypeStruct((1,), jnp.int32),
        ),
        in_specs=[pl.BlockSpec(memory_space=pl.ANY), pl.BlockSpec(memory_space=pl.ANY), smem],
        out_specs=(vmem, smem, smem),
        scratch_shapes=[
            pltpu.VMEM((2, TOK, width), jnp.bfloat16),
            pltpu.VMEM((TOK, width), jnp.bfloat16),
            pltpu.SMEM((HEADS,), jnp.int32),
            pltpu.SemaphoreType.DMA((3,)),
        ],
    )(queries.reshape(TOK, width), key_value.reshape(2, TOK, width), windows.T)
    branches = [functools.partial(attend, i, n_frame, n_chip_y) for i in range(len(PLANS))]
    slots = lax.switch(choice[0], branches, packed, flags)
    result = pl.pallas_call(
        place_kernel,
        out_shape=jax.ShapeDtypeStruct((TOK, width), jnp.bfloat16),
        in_specs=[vmem, smem],
        out_specs=vmem,
    )(slots, flags)
    return result.reshape(queries.shape)


def solution(mesh):
    in_specs = (
        P(("cand", "frame"), "height", None, None),
        P(None, ("cand", "frame"), "height", None, None),
        P(),
    )
    out_specs = P(("cand", "frame"), "height", None, None)
    return jax.shard_map(shards, mesh=mesh, in_specs=in_specs, out_specs=out_specs, check_vma=False)
```

```python
import functools
import math

import jax
import jax.numpy as jnp
from jax import lax
from jax.experimental import pallas as pl
from jax.experimental.pallas import tpu as pltpu
from jax.sharding import PartitionSpec as P

HEADS = 12
HALF = HEADS // 2
HD = 128
TOK = 128
CHIP = 2 * TOK
W = 16
TW = 8
NEG = -1e30
EXTRA = 16
SCALE = math.log2(math.e) / math.sqrt(HD)
MESH = pl.DeviceIdType.MESH


def dot(a, b, dims):
    return lax.dot_general(a, b, ((dims[0], dims[1]), ((), ())), preferred_element_type=jnp.float32)


PLANS = (
    (4, 2, 10),
    (4, 0, 8),
    (5, 2, 10),
    (6, 2, 10),
    (5, 0, 10),
    (7, 2, 12),
    (8, 2, 12),
    (7, 0, 12),
    (9, 2, 12),
    (12, 0, 12),
)


def sort_kernel(q, kv, win, packed, flags, choice):
    wf = [win[0, h] for h in range(HEADS)]
    wh = [win[1, h] for h in range(HEADS)]
    kinds = [(a - a * b, a * b, b - a * b, (1 - a) * (1 - b)) for a, b in zip(wf, wh)]
    count = [sum(kind[i] for kind in kinds) for i in range(4)]
    free = [jnp.int32(0), count[0], count[0] + count[1], count[0] + count[1] + count[2]]
    ranks = []
    for kind in kinds:
        ranks.append(sum(x * place for x, place in zip(kind, free)))
        free = [place + x for x, place in zip(kind, free)]
    heads = [sum(jnp.where(ranks[h] == s, h, 0) for h in range(HEADS)) for s in range(HEADS)]
    wide, lone, tall = count[0] + count[1], count[0], count[1] + count[2]
    best = jnp.int32(len(PLANS) - 1)
    for i in reversed(range(len(PLANS) - 1)):
        nf, h0, h1 = PLANS[i]
        best = jnp.where((wide <= nf) & (lone >= h0) & (lone + tall <= h1), i, best)
    choice[0] = best
    for s in range(HEADS):
        for i in range(3):
            flags[s, i] = win[i, heads[s]]
        flags[s, 3] = ranks[s]
        columns = pl.ds(pl.multiple_of(heads[s] * HD, HD), HD)
        packed[s % 2, s // 2, 0] = kv[0, :, columns]
        packed[s % 2, s // 2, 1] = kv[1, :, columns].T
        packed[s % 2, s // 2, 2] = q[:, columns]


def place_kernel(o, flags, out):
    for h in range(HEADS):
        out[:, h * HD : (h + 1) * HD] = o[flags[h, 3]]


def kernel(
    cfg,
    n_frame,
    n_chip_y,
    packed,
    flags,
    out,
    kv,
    qa,
    acc,
    top,
    rs,
    rr,
    oh,
    own_l,
    own_s,
    own_r,
    z_s,
    z_r,
    q_s,
    q_r,
    ret_s,
    ret_r,
    o_l,
    o_s,
    o_r,
):
    nf, h0, h1 = cfg
    lo, hi = h0 // 2, h1 // 2
    f = lax.axis_index("frame")
    height = lax.axis_index("height")
    y = height // 2
    c = height % 2
    other = 1 - c
    z_ok = (f > 0, f < n_frame - 1)
    y_ok = (y > 0, y < n_chip_y - 1)
    z_dev = (f - 1, f + 1)
    y_dev = (y - 1, y + 1)
    partner = {"height": 2 * y + other}

    barrier = pltpu.get_barrier_semaphore()
    pl.semaphore_signal(barrier, inc=1, device_id=partner, device_id_type=MESH)
    for d in range(2):

        @pl.when(z_ok[d])
        def _():
            for g in range(2):
                pl.semaphore_signal(
                    barrier,
                    inc=1,
                    device_id={"frame": z_dev[d], "height": 2 * y + g},
                    device_id_type=MESH,
                )

        @pl.when(y_ok[d])
        def _():
            for g in range(2):
                pl.semaphore_signal(
                    barrier,
                    inc=1,
                    device_id={"height": 2 * y_dev[d] + g},
                    device_id_type=MESH,
                )

    own_loads = (
        pltpu.make_async_copy(packed.at[c, :, pl.ds(0, 2)], kv.at[1, :, c], own_l.at[0]),
        pltpu.make_async_copy(packed.at[c, :, 2], qa.at[:, 0, c], own_l.at[1]),
    )

    def remote(src, dst, send_sem, recv_sem, device):
        return pltpu.make_async_remote_copy(
            src_ref=src,
            dst_ref=dst,
            send_sem=send_sem,
            recv_sem=recv_sem,
            device_id=device,
            device_id_type=MESH,
        )

    own_copies = (
        remote(
            packed.at[other, :, pl.ds(0, 2)], kv.at[1, :, c], own_s.at[0], own_r.at[0], partner
        ),
        remote(packed.at[other, :, 2], qa.at[:, 0, c], own_s.at[1], own_r.at[1], partner),
    )

    def z_copy(d, j, g):
        return remote(
            packed.at[g, j, pl.ds(0, 2)],
            kv.at[2 - 2 * d, j, c],
            z_s.at[d, j, g],
            z_r.at[1 - d, j, c],
            {"frame": z_dev[d], "height": 2 * y + g},
        )

    def z_arrival(d, j, half):
        dst = kv.at[2 * d, j, half]
        return remote(dst, dst, z_s.at[d, j, 0], z_r.at[d, j, half], partner)

    def q_copy(d, j, g):
        return remote(
            packed.at[g, j, 2],
            qa.at[j, 2 - d, c],
            q_s.at[d, j, g],
            q_r.at[1 - d, j, c],
            {"height": 2 * y_dev[d] + g},
        )

    def q_arrival(d, j, half):
        dst = qa.at[j, 1 + d, half]
        return remote(dst, dst, q_s.at[d, j, 0], q_r.at[d, j, half], partner)

    def ret_copy(d, j):
        return remote(
            rs.at[d, j],
            rr.at[1 - d, j],
            ret_s.at[d, j],
            ret_r.at[1 - d, j],
            {"height": 2 * y_dev[d] + c},
        )

    def o_copy(j):
        return remote(oh.at[j, other], out.at[2 * j + c], o_s.at[j], o_r.at[j], partner)

    def o_arrival(j):
        dst = out.at[2 * j + other]
        return remote(dst, dst, o_s.at[j], o_r.at[j], partner)

    def o_store(j):
        return pltpu.make_async_copy(oh.at[j, c], out.at[2 * j + c], o_l.at[j])

    for copy in own_loads:
        copy.start()

    for d in range(2):

        @pl.when(jnp.logical_not(y_ok[d]))
        def _():
            rr[d] = jnp.zeros(rr.shape[1:], rr.dtype)

        @pl.when(jnp.logical_not(z_ok[d]))
        def _():
            kv[2 * d] = jnp.zeros(kv.shape[1:], kv.dtype)

    pl.semaphore_wait(
        barrier,
        1
        + 2 * sum(jnp.where(ok, 1, 0) for ok in z_ok)
        + 2 * sum(jnp.where(ok, 1, 0) for ok in y_ok),
    )

    def send_z(slots):
        for d in range(2):

            @pl.when(z_ok[d])
            def _():
                for s in slots:
                    z_copy(d, s // 2, s % 2).start()

    z_order = tuple(reversed(range(nf)))
    for copy in own_copies:
        copy.start()
    send_z(z_order[:4])
    few, most = nf // 2, (nf + 1) // 2

    @pl.loop(lo, hi)
    def _(n):
        j = jnp.where(n < most, most - 1 - n + lo, n)
        for d in range(2):

            @pl.when(y_ok[d])
            def _():
                for g in range(2):
                    q_copy(d, j, g).start()

    key_side = lax.broadcasted_iota(jnp.int32, (W, 3 * CHIP), 0) // TW
    query_side = lax.broadcasted_iota(jnp.int32, (W, 3 * CHIP), 1) % W // TW
    apart = jnp.where(key_side == query_side, 0.0, NEG).astype(jnp.float32)
    ones = jnp.ones((EXTRA, CHIP), jnp.bfloat16)

    def shut(j, column):
        return (1 - flags[2 * j + c, column]).astype(jnp.float32)

    def keys(tile, j):
        return kv[tile, j, :, 0].reshape(CHIP, HD)

    def values(tile, j):
        vt = jnp.concatenate([kv[tile, j, 0, 1], kv[tile, j, 1, 1]], axis=1)
        return jnp.concatenate([vt, ones], axis=0)

    def scores(k, j, parts):
        q = qa[j, 0:parts].reshape(parts * CHIP, HD)
        return dot(k, q, ((1,), (1,)))

    def weights(s, m):
        return jnp.exp2((s - m) * SCALE).astype(jnp.bfloat16)

    def here(j, parts):
        n = parts * CHIP
        s = scores(keys(1, j), j, parts)
        bias = apart[:, :n] * shut(j, 2)
        s = (s.reshape(CHIP // W, W, n) + bias[None]).reshape(CHIP, n)
        m = jnp.max(s, axis=0, keepdims=True)
        top[j, 0:1, 0:n] = m
        acc[j, :, 0:n] = dot(values(1, j), weights(s, m), ((1,), (0,)))

    def around(j, parts):
        for d in range(2):

            @pl.when(z_ok[d])
            def _():
                for half in range(2):
                    z_arrival(d, j, half).wait_recv()

        n = parts * CHIP
        s = scores(jnp.concatenate([keys(0, j), keys(2, j)], axis=0), j, parts)
        width = apart[:, :n] * shut(j, 2)
        closed = shut(j, 0) * NEG
        bias = jnp.stack([width + jnp.where(z_ok[d], closed, NEG) for d in range(2)])[:, None]
        s = (s.reshape(2, CHIP // W, W, n) + bias).reshape(2 * CHIP, n)
        m_old = top[j, 0:1, 0:n]
        m = jnp.maximum(m_old, jnp.max(s, axis=0, keepdims=True))
        vt = jnp.concatenate([values(0, j), values(2, j)], axis=1)
        fade = jnp.exp2((m_old - m) * SCALE)
        top[j, 0:1, 0:n] = m
        acc[j, :, 0:n] = acc[j, :, 0:n] * fade + dot(vt, weights(s, m), ((1,), (0,)))

    def give_back(j):
        n = slice(CHIP, 3 * CHIP)
        m = top[j, 0:1, n]
        total = acc[j, HD : HD + 1, n]
        o = (acc[j, 0:HD, n] * (1.0 / total)).astype(jnp.bfloat16)
        level = m * SCALE + jnp.log2(total)
        a = level.astype(jnp.bfloat16).astype(jnp.float32)
        b = (level - a).astype(jnp.bfloat16).astype(jnp.float32)
        row = lax.broadcasted_iota(jnp.int32, (EXTRA, 2 * CHIP), 0)
        rest = jnp.where(row == 2, level - a - b, 0.0)
        digits = jnp.where(row == 0, a, jnp.where(row == 1, b, rest)).astype(jnp.bfloat16)
        for d in range(2):
            rs[d, j, 0:HD] = o[:, d * CHIP : (d + 1) * CHIP]
            rs[d, j, HD : HD + EXTRA] = digits[:, d * CHIP : (d + 1) * CHIP]
        for d in range(2):

            @pl.when(y_ok[d])
            def _():
                ret_copy(d, j).start()

    def finish(j, o):
        o = o.T.astype(jnp.bfloat16)
        oh[j, 0] = o[:TOK]
        oh[j, 1] = o[TOK:]
        o_copy(j).start()
        o_store(j).start()

    def alone(j):
        finish(j, acc[j, 0:HD, 0:CHIP] * (1.0 / acc[j, HD : HD + 1, 0:CHIP]))

    def join(j):
        for d in range(2):

            @pl.when(y_ok[d])
            def _():
                ret_copy(1 - d, j).wait_recv()

        m = top[j, 0:1, 0:CHIP] * SCALE
        total = acc[j, HD : HD + 1, 0:CHIP]
        low = shut(j, 1) * NEG
        levels = []
        for d in range(2):
            digits = rr[d, j, HD : HD + EXTRA].astype(jnp.float32)
            level = jnp.sum(digits, axis=0, keepdims=True)
            levels.append(level + jnp.where(y_ok[d], low, NEG))
        best = jnp.maximum(m + jnp.log2(total), jnp.maximum(levels[0], levels[1]))
        w = [jnp.exp2(x - best) for x in (m, *levels)]
        over = 1.0 / (total * w[0] + w[1] + w[2])
        o = acc[j, 0:HD, 0:CHIP] * (w[0] * over)
        for d in range(2):
            o = o + rr[d, j, 0:HD].astype(jnp.float32) * (w[d + 1] * over)
        finish(j, o)

    for copy in own_loads:
        copy.wait()
    for copy in own_copies:
        copy.wait_recv()

    if lo + HALF - hi > 0:

        @pl.loop(0, lo + HALF - hi)
        def _(n):
            j = jnp.where(n < lo, n, n - lo + hi)
            here(j, 1)

            @pl.when(j >= hi)
            def _():
                alone(j)

    send_z(z_order[4:])

    my_z = (nf + 1 - c) // 2
    n_in = my_z - lo
    n_out = hi - my_z

    @pl.loop(0, 2 * n_in + n_out)
    def _(n):
        outer = (n == n_in) | (n > n_in + n_out)
        j_in = jnp.where(n < n_in, my_z - 1 - n, my_z - 1 + n - n_in)
        j_out = jnp.where(n == n_in, my_z - 1, my_z - 1 - (n - n_in - n_out))
        j = jnp.where(outer, j_out, j_in)

        @pl.when(jnp.logical_not(outer))
        def _():
            for d in range(2):

                @pl.when(y_ok[d])
                def _():
                    for half in range(2):
                        q_arrival(d, j, half).wait_recv()

            here(j, 3)

        @pl.when(outer)
        def _():
            around(j, 3)

        @pl.when(n >= n_in)
        def _():
            give_back(j)

    for copy in own_copies:
        copy.wait_send()

    if lo > 0:

        @pl.loop(0, lo)
        def _(j):
            around(j, 1)
            alone(j)

    @pl.loop(0, hi - lo)
    def _(n):
        join(jnp.where(n < n_out, my_z + n, my_z - 1 - (n - n_out)))

    for d in range(2):

        @pl.when(z_ok[d])
        def _():
            for s in range(nf):
                z_copy(d, s // 2, s % 2).wait_send()

        @pl.when(y_ok[d])
        def _():
            @pl.loop(lo, hi)
            def _(j):
                for g in range(2):
                    q_copy(d, j, g).wait_send()
                ret_copy(d, j).wait_send()

    @pl.loop(0, HALF)
    def _(j):
        o_store(j).wait()
        o_copy(j).wait_send()
        o_arrival(j).wait_recv()


def attend(index, n_frame, n_chip_y, packed, flags):
    nf, h0, h1 = PLANS[index]
    assert h0 % 2 == 0 and h1 % 2 == 0 and h0 < nf - 1 and nf <= h1
    bf16, f32 = jnp.bfloat16, jnp.float32
    dma = pltpu.SemaphoreType.DMA
    return pl.pallas_call(
        functools.partial(kernel, PLANS[index], n_frame, n_chip_y),
        out_shape=jax.ShapeDtypeStruct((HEADS, TOK, HD), bf16),
        in_specs=[pl.BlockSpec(memory_space=pl.ANY), pl.BlockSpec(memory_space=pltpu.SMEM)],
        out_specs=pl.BlockSpec(memory_space=pl.ANY),
        scratch_shapes=[
            pltpu.VMEM((3, HALF, 2, 2, TOK, HD), bf16),
            pltpu.VMEM((HALF, 3, 2, TOK, HD), bf16),
            pltpu.VMEM((HALF, HD + EXTRA, 3 * CHIP), f32),
            pltpu.VMEM((HALF, 8, 3 * CHIP), f32),
            pltpu.VMEM((2, HALF, HD + EXTRA, CHIP), bf16),
            pltpu.VMEM((2, HALF, HD + EXTRA, CHIP), bf16),
            pltpu.VMEM((HALF, 2, TOK, HD), bf16),
            dma((2,)),
            dma((2,)),
            dma((2,)),
            dma((2, HALF, 2)),
            dma((2, HALF, 2)),
            dma((2, HALF, 2)),
            dma((2, HALF, 2)),
            dma((2, HALF)),
            dma((2, HALF)),
            dma((HALF,)),
            dma((HALF,)),
            dma((HALF,)),
        ],
        compiler_params=pltpu.CompilerParams(
            collective_id=index,
            has_side_effects=True,
            vmem_limit_bytes=32 * 1024 * 1024,
        ),
    )(packed, flags)


def shards(queries, key_value, windows):
    n_frame = lax.axis_size("frame")
    n_chip_y = lax.axis_size("height") // 2
    width = HEADS * HD
    vmem = pl.BlockSpec(memory_space=pltpu.VMEM)
    smem = pl.BlockSpec(memory_space=pltpu.SMEM)
    packed, flags, choice = pl.pallas_call(
        sort_kernel,
        out_shape=(
            jax.ShapeDtypeStruct((2, HALF, 3, TOK, HD), jnp.bfloat16),
            jax.ShapeDtypeStruct((HEADS, 4), jnp.int32),
            jax.ShapeDtypeStruct((1,), jnp.int32),
        ),
        in_specs=[vmem, vmem, smem],
        out_specs=(vmem, smem, smem),
    )(queries.reshape(TOK, width), key_value.reshape(2, TOK, width), windows.T)
    branches = [functools.partial(attend, i, n_frame, n_chip_y) for i in range(len(PLANS))]
    slots = lax.switch(choice[0], branches, packed, flags)
    result = pl.pallas_call(
        place_kernel,
        out_shape=jax.ShapeDtypeStruct((TOK, width), jnp.bfloat16),
        in_specs=[vmem, smem],
        out_specs=vmem,
    )(slots, flags)
    return result.reshape(queries.shape)


def solution(mesh):
    in_specs = (
        P(("cand", "frame"), "height", None, None),
        P(None, ("cand", "frame"), "height", None, None),
        P(),
    )
    out_specs = P(("cand", "frame"), "height", None, None)
    return jax.shard_map(shards, mesh=mesh, in_specs=in_specs, out_specs=out_specs, check_vma=False)
```

```python
import functools
import math

import jax
import jax.numpy as jnp
from jax import lax
from jax.experimental import pallas as pl
from jax.experimental.pallas import tpu as pltpu
from jax.sharding import PartitionSpec as P

HEADS = 12
HALF = HEADS // 2
HD = 128
TOK = 128
CHIP = 2 * TOK
W = 16
TW = 8
NEG = -1e30
EXTRA = 16
SCALE = math.log2(math.e) / math.sqrt(HD)
MESH = pl.DeviceIdType.MESH


def dot(a, b, dims):
    return lax.dot_general(a, b, ((dims[0], dims[1]), ((), ())), preferred_element_type=jnp.float32)


PLANS = (
    (4, 5, 2),
    (5, 6, 3),
    (5, 7, 2),
    (6, 7, 4),
    (6, 8, 3),
    (7, 8, 5),
    (7, 9, 4),
    (8, 9, 6),
    (9, 10, 7),
    (12, 12, 12),
)


def sort_kernel(q, kv, win, packed, flags, choice):
    wf = [win[0, h] for h in range(HEADS)]
    wh = [win[1, h] for h in range(HEADS)]
    kinds = [(a - a * b, a * b, b - a * b, (1 - a) * (1 - b)) for a, b in zip(wf, wh)]
    lone, two, tall, _ = [sum(kind[i] for kind in kinds) for i in range(4)]
    best, start, end = jnp.int32(len(PLANS) - 1), jnp.int32(0), jnp.int32(HEADS)
    for i in reversed(range(len(PLANS) - 1)):
        nf, nh, both = PLANS[i]
        fits = (lone + two <= nf) & (two + tall <= nh) & (two <= both)
        fits = fits & (lone + two + tall <= nf + nh - both)
        best = jnp.where(fits, i, best)
        start = jnp.where(fits, nf - both, start)
        end = jnp.where(fits, nf - both + nh, end)
    choice[0] = best
    middle = jnp.maximum(start, lone)
    gap = middle - lone
    after = end - tall - middle - two
    free = [jnp.int32(0), middle, end - 1, jnp.int32(0)]
    ranks = []
    for kind in kinds:
        i = free[3]
        rest = jnp.where(i < gap, lone + i, jnp.where(i < gap + after, middle + two - gap + i, end - gap - after + i))
        ranks.append(kind[0] * free[0] + kind[1] * free[1] + kind[2] * free[2] + kind[3] * rest)
        free = [free[0] + kind[0], free[1] + kind[1], free[2] - kind[2], free[3] + kind[3]]
    heads = [sum(jnp.where(ranks[h] == s, h, 0) for h in range(HEADS)) for s in range(HEADS)]
    for s in range(HEADS):
        for i in range(3):
            flags[s, i] = win[i, heads[s]]
        flags[s, 3] = ranks[s] % 2 * HALF + ranks[s] // 2
        columns = pl.ds(pl.multiple_of(heads[s] * HD, HD), HD)
        at = s % 2 * HALF + s // 2
        packed[0, at] = kv[0, :, columns]
        packed[1, at] = kv[1, :, columns].T
        packed[2, at] = q[:, columns]


def place_kernel(o, flags, out):
    for h in range(HEADS):
        out[:, h * HD : (h + 1) * HD] = o[flags[h, 3]]


def kernel(
    cfg,
    n_frame,
    n_chip_y,
    packed,
    flags,
    out,
    kv,
    qa,
    acc,
    top,
    rs,
    rr,
    oh,
    own_l,
    own_s,
    own_r,
    z_s,
    z_r,
    q_s,
    q_r,
    ret_s,
    ret_r,
    o_l,
    o_s,
    o_r,
):
    nf, nh, both = cfg
    h0 = nf - both
    h1 = h0 + nh

    def part(start, end, g):
        return (start + 1 - g) // 2, (end + 1 - g) // 2

    f = lax.axis_index("frame")
    height = lax.axis_index("height")
    y = height // 2
    c = height % 2
    other = 1 - c
    z_ok = (f > 0, f < n_frame - 1)
    y_ok = (y > 0, y < n_chip_y - 1)
    z_dev = (f - 1, f + 1)
    y_dev = (y - 1, y + 1)
    partner = {"height": 2 * y + other}

    barrier = pltpu.get_barrier_semaphore()
    pl.semaphore_signal(barrier, inc=1, device_id=partner, device_id_type=MESH)
    for d in range(2):

        @pl.when(z_ok[d])
        def _():
            for g in range(2):
                pl.semaphore_signal(
                    barrier,
                    inc=1,
                    device_id={"frame": z_dev[d], "height": 2 * y + g},
                    device_id_type=MESH,
                )

        @pl.when(y_ok[d])
        def _():
            for g in range(2):
                pl.semaphore_signal(
                    barrier,
                    inc=1,
                    device_id={"height": 2 * y_dev[d] + g},
                    device_id_type=MESH,
                )

    own_loads = (
        pltpu.make_async_copy(
            packed.at[pl.ds(0, 2), pl.ds(c * HALF, HALF)], kv.at[1, :, :, c], own_l.at[0]
        ),
        pltpu.make_async_copy(packed.at[2, pl.ds(c * HALF, HALF)], qa.at[:, 0, c], own_l.at[1]),
    )

    def remote(src, dst, send_sem, recv_sem, device):
        return pltpu.make_async_remote_copy(
            src_ref=src,
            dst_ref=dst,
            send_sem=send_sem,
            recv_sem=recv_sem,
            device_id=device,
            device_id_type=MESH,
        )

    own_copies = (
        remote(
            packed.at[pl.ds(0, 2), pl.ds(other * HALF, HALF)],
            kv.at[1, :, :, c],
            own_s.at[0],
            own_r.at[0],
            partner,
        ),
        remote(
            packed.at[2, pl.ds(other * HALF, HALF)],
            qa.at[:, 0, c],
            own_s.at[1],
            own_r.at[1],
            partner,
        ),
    )

    def z_copy(d, s):
        j, g = s // 2, s % 2
        return remote(
            packed.at[pl.ds(0, 2), g * HALF + j],
            kv.at[2 - 2 * d, :, j, c],
            z_s.at[d],
            z_r.at[1 - d, j],
            {"frame": z_dev[d], "height": 2 * y + g},
        )

    def z_arrival(d, j):
        dst = kv.at[2 * d, :, j]
        return remote(dst, dst, z_s.at[d], z_r.at[d, j], partner)

    def z_sent(d):
        src = packed.at[pl.ds(0, 2), pl.ds(0, nf)]
        return remote(src, src, z_s.at[d], z_r.at[d, 0], partner)

    runs = ((nf, h1), (h0, nf))

    def q_copy(d, i, g):
        j, end = part(*runs[i], g)
        return remote(
            packed.at[2, pl.ds(g * HALF + j, end - j)],
            qa.at[pl.ds(j, end - j), 2 - d, c],
            q_s.at[d],
            q_r.at[1 - d, i],
            {"height": 2 * y_dev[d] + g},
        )

    def q_arrival(d, i, g):
        j, end = part(*runs[i], g)
        dst = qa.at[pl.ds(j, end - j), 1 + d]
        return remote(dst, dst, q_s.at[d], q_r.at[d, i], partner)

    def q_sent(d):
        src = packed.at[2, pl.ds(0, nh)]
        return remote(src, src, q_s.at[d], q_r.at[d, 0], partner)

    def filled(i, g):
        j, end = part(*runs[i], g)
        return j < end

    def ret_copy(d, j):
        return remote(
            rs.at[d, j],
            rr.at[1 - d, j],
            ret_s.at[d, j],
            ret_r.at[1 - d, j],
            {"height": 2 * y_dev[d] + c},
        )

    def o_copy(j):
        return remote(oh.at[other, j], out.at[c * HALF + j], o_s, o_r, partner)

    def o_arrivals():
        return remote(oh.at[other], out.at[pl.ds(other * HALF, HALF)], o_s, o_r, partner)

    def o_store(j):
        return pltpu.make_async_copy(oh.at[c, j], out.at[c * HALF + j], o_l)

    def o_stores():
        return pltpu.make_async_copy(oh.at[c], out.at[pl.ds(c * HALF, HALF)], o_l)

    for copy in own_loads:
        copy.start()

    for d in range(2):

        @pl.when(jnp.logical_not(y_ok[d]))
        def _():
            rr[d] = jnp.zeros(rr.shape[1:], rr.dtype)

        @pl.when(jnp.logical_not(z_ok[d]))
        def _():
            kv[2 * d] = jnp.zeros(kv.shape[1:], kv.dtype)

    pl.semaphore_wait(
        barrier,
        1
        + 2 * sum(jnp.where(ok, 1, 0) for ok in z_ok)
        + 2 * sum(jnp.where(ok, 1, 0) for ok in y_ok),
    )

    def send_z(slots):
        for d in range(2):

            @pl.when(z_ok[d])
            def _():
                for s in slots:
                    z_copy(d, s).start()

    z_order = tuple(reversed(range(nf)))
    for copy in own_copies:
        copy.start()
    send_z(z_order[:4])
    for i in range(2):
        for d in range(2):

            @pl.when(y_ok[d])
            def _():
                for g in range(2):
                    if filled(i, g):
                        q_copy(d, i, g).start()

    key_side = lax.broadcasted_iota(jnp.int32, (W, 3 * CHIP), 0) // TW
    query_side = lax.broadcasted_iota(jnp.int32, (W, 3 * CHIP), 1) % W // TW
    apart = jnp.where(key_side == query_side, 0.0, NEG).astype(jnp.float32)
    ones = jnp.ones((EXTRA, CHIP), jnp.bfloat16)

    def shut(j, column):
        return (1 - flags[2 * j + c, column]).astype(jnp.float32)

    def keys(tile, j):
        return kv[tile, 0, j].reshape(CHIP, HD)

    def values(tile, j):
        vt = jnp.concatenate([kv[tile, 1, j, 0], kv[tile, 1, j, 1]], axis=1)
        return jnp.concatenate([vt, ones], axis=0)

    def scores(k, j, parts):
        q = qa[j, 0:parts].reshape(parts * CHIP, HD)
        return dot(k, q, ((1,), (1,)))

    def weights(s, m):
        return jnp.exp2((s - m) * SCALE).astype(jnp.bfloat16)

    def here(j, parts):
        n = parts * CHIP
        s = scores(keys(1, j), j, parts)
        bias = apart[:, :n] * shut(j, 2)
        s = (s.reshape(CHIP // W, W, n) + bias[None]).reshape(CHIP, n)
        m = jnp.max(s, axis=0, keepdims=True)
        top[j, 0:1, 0:n] = m
        acc[j, :, 0:n] = dot(values(1, j), weights(s, m), ((1,), (0,)))

    def around(j, parts):
        for d in range(2):

            @pl.when(z_ok[d])
            def _():
                z_arrival(d, j).wait_recv()

        n = parts * CHIP
        s = scores(jnp.concatenate([keys(0, j), keys(2, j)], axis=0), j, parts)
        width = apart[:, :n] * shut(j, 2)
        closed = shut(j, 0) * NEG
        bias = jnp.stack([width + jnp.where(z_ok[d], closed, NEG) for d in range(2)])[:, None]
        s = (s.reshape(2, CHIP // W, W, n) + bias).reshape(2 * CHIP, n)
        m_old = top[j, 0:1, 0:n]
        m = jnp.maximum(m_old, jnp.max(s, axis=0, keepdims=True))
        vt = jnp.concatenate([values(0, j), values(2, j)], axis=1)
        fade = jnp.exp2((m_old - m) * SCALE)
        top[j, 0:1, 0:n] = m
        acc[j, :, 0:n] = acc[j, :, 0:n] * fade + dot(vt, weights(s, m), ((1,), (0,)))

    def give_back(j):
        n = slice(CHIP, 3 * CHIP)
        m = top[j, 0:1, n]
        total = acc[j, HD : HD + 1, n]
        o = (acc[j, 0:HD, n] * (1.0 / total)).astype(jnp.bfloat16)
        level = m * SCALE + jnp.log2(total)
        a = level.astype(jnp.bfloat16).astype(jnp.float32)
        b = (level - a).astype(jnp.bfloat16).astype(jnp.float32)
        row = lax.broadcasted_iota(jnp.int32, (EXTRA, 2 * CHIP), 0)
        rest = jnp.where(row == 2, level - a - b, 0.0)
        digits = jnp.where(row == 0, a, jnp.where(row == 1, b, rest)).astype(jnp.bfloat16)
        for d in range(2):
            rs[d, j, 0:HD] = o[:, d * CHIP : (d + 1) * CHIP]
            rs[d, j, HD : HD + EXTRA] = digits[:, d * CHIP : (d + 1) * CHIP]
        for d in range(2):

            @pl.when(y_ok[d])
            def _():
                ret_copy(d, j).start()

    def finish(j, o):
        o = o.T.astype(jnp.bfloat16)
        oh[0, j] = o[:TOK]
        oh[1, j] = o[TOK:]
        o_copy(j).start()
        o_store(j).start()

    def alone(j):
        finish(j, acc[j, 0:HD, 0:CHIP] * (1.0 / acc[j, HD : HD + 1, 0:CHIP]))

    def join(j):
        for d in range(2):

            @pl.when(y_ok[d])
            def _():
                ret_copy(1 - d, j).wait_recv()
                ret_copy(d, j).wait_send()

        m = top[j, 0:1, 0:CHIP] * SCALE
        total = acc[j, HD : HD + 1, 0:CHIP]
        low = shut(j, 1) * NEG
        levels = []
        for d in range(2):
            digits = rr[d, j, HD : HD + EXTRA].astype(jnp.float32)
            level = jnp.sum(digits, axis=0, keepdims=True)
            levels.append(level + jnp.where(y_ok[d], low, NEG))
        best = jnp.maximum(m + jnp.log2(total), jnp.maximum(levels[0], levels[1]))
        w = [jnp.exp2(x - best) for x in (m, *levels)]
        over = 1.0 / (total * w[0] + w[1] + w[2])
        o = acc[j, 0:HD, 0:CHIP] * (w[0] * over)
        for d in range(2):
            o = o + rr[d, j, 0:HD].astype(jnp.float32) * (w[d + 1] * over)
        finish(j, o)

    for copy in own_loads:
        copy.wait()
    for copy in own_copies:
        copy.wait_recv()

    lo, hi = part(h0, h1, c)
    my_z = part(0, nf, c)[1]
    n_in = my_z - lo
    n_out = hi - my_z

    @pl.loop(0, lo + HALF - hi)
    def _(n):
        j = jnp.where(n < lo, n, n - lo + hi)
        here(j, 1)

        @pl.when(j >= hi)
        def _():
            alone(j)

    send_z(z_order[4:])

    @pl.loop(0, n_out + 2 * n_in)
    def _(n):
        outer = n >= n_out + n_in
        j = jnp.where(n < n_out, my_z + n, my_z - 1 - (n - n_out) + jnp.where(outer, n_in, 0))
        for i in range(2):
            for d in range(2):
                for g in range(2):
                    if filled(i, g):

                        @pl.when((n == (n_out if i else 0)) & (c == g) & y_ok[d])
                        def _():
                            q_arrival(d, i, g).wait_recv()

        @pl.when(jnp.logical_not(outer))
        def _():
            here(j, 3)

        @pl.when(outer)
        def _():
            around(j, 3)

        @pl.when(outer | (n < n_out))
        def _():
            give_back(j)

    if h0 > 0:

        @pl.loop(0, lo)
        def _(j):
            around(j, 1)
            alone(j)

    for copy in own_copies:
        copy.wait_send()
    for d in range(2):

        @pl.when(z_ok[d])
        def _():
            z_sent(d).wait_send()

        @pl.when(y_ok[d])
        def _():
            q_sent(d).wait_send()

    @pl.loop(0, hi - lo)
    def _(n):
        join(jnp.where(n < n_out, my_z + n, my_z - 1 - (n - n_out)))

    o_stores().wait()
    o_arrivals().wait()


def attend(index, n_frame, n_chip_y, packed, flags):
    nf, nh, both = PLANS[index]
    assert both <= min(nf, nh) and nf + nh - both <= HEADS
    bf16, f32 = jnp.bfloat16, jnp.float32
    dma = pltpu.SemaphoreType.DMA
    return pl.pallas_call(
        functools.partial(kernel, PLANS[index], n_frame, n_chip_y),
        out_shape=jax.ShapeDtypeStruct((HEADS, TOK, HD), bf16),
        in_specs=[pl.BlockSpec(memory_space=pl.ANY), pl.BlockSpec(memory_space=pltpu.SMEM)],
        out_specs=pl.BlockSpec(memory_space=pl.ANY),
        scratch_shapes=[
            pltpu.VMEM((3, 2, HALF, 2, TOK, HD), bf16),
            pltpu.VMEM((HALF, 3, 2, TOK, HD), bf16),
            pltpu.VMEM((HALF, HD + EXTRA, 3 * CHIP), f32),
            pltpu.VMEM((HALF, 8, 3 * CHIP), f32),
            pltpu.VMEM((2, HALF, HD + EXTRA, CHIP), bf16),
            pltpu.VMEM((2, HALF, HD + EXTRA, CHIP), bf16),
            pltpu.VMEM((2, HALF, TOK, HD), bf16),
            dma((2,)),
            dma((2,)),
            dma((2,)),
            dma((2,)),
            dma((2, HALF)),
            dma((2,)),
            dma((2, 2)),
            dma((2, HALF)),
            dma((2, HALF)),
            dma,
            dma,
            dma,
        ],
        compiler_params=pltpu.CompilerParams(
            collective_id=index,
            has_side_effects=True,
            vmem_limit_bytes=32 * 1024 * 1024,
        ),
    )(packed, flags)


def shards(queries, key_value, windows):
    n_frame = lax.axis_size("frame")
    n_chip_y = lax.axis_size("height") // 2
    width = HEADS * HD
    vmem = pl.BlockSpec(memory_space=pltpu.VMEM)
    smem = pl.BlockSpec(memory_space=pltpu.SMEM)
    packed, flags, choice = pl.pallas_call(
        sort_kernel,
        out_shape=(
            jax.ShapeDtypeStruct((3, HEADS, TOK, HD), jnp.bfloat16),
            jax.ShapeDtypeStruct((HEADS, 4), jnp.int32),
            jax.ShapeDtypeStruct((1,), jnp.int32),
        ),
        in_specs=[vmem, vmem, smem],
        out_specs=(vmem, smem, smem),
    )(queries.reshape(TOK, width), key_value.reshape(2, TOK, width), windows.T)
    branches = [functools.partial(attend, i, n_frame, n_chip_y) for i in range(len(PLANS))]
    slots = lax.switch(choice[0], branches, packed, flags)
    result = pl.pallas_call(
        place_kernel,
        out_shape=jax.ShapeDtypeStruct((TOK, width), jnp.bfloat16),
        in_specs=[vmem, smem],
        out_specs=vmem,
    )(slots, flags)
    return result.reshape(queries.shape)


def solution(mesh):
    in_specs = (
        P(("cand", "frame"), "height", None, None),
        P(None, ("cand", "frame"), "height", None, None),
        P(),
    )
    out_specs = P(("cand", "frame"), "height", None, None)
    return jax.shard_map(shards, mesh=mesh, in_specs=in_specs, out_specs=out_specs, check_vma=False)
```

```python
import functools
import math

import jax
import jax.numpy as jnp
from jax import lax
from jax.experimental import pallas as pl
from jax.experimental.pallas import tpu as pltpu
from jax.sharding import PartitionSpec as P

HEADS = 12
HALF = HEADS // 2
HD = 128
TOK = 128
CHIP = 2 * TOK
W = 16
TW = 8
NEG = -1e30
EXTRA = 16
SCALE = math.log2(math.e) / math.sqrt(HD)
MESH = pl.DeviceIdType.MESH


def dot(a, b, dims):
    return lax.dot_general(a, b, ((dims[0], dims[1]), ((), ())), preferred_element_type=jnp.float32)


PLANS = (
    (4, 5, 2),
    (5, 6, 3),
    (5, 7, 2),
    (6, 7, 4),
    (6, 8, 3),
    (7, 8, 5),
    (7, 9, 4),
    (8, 9, 6),
    (9, 10, 7),
    (12, 12, 12),
)


def sort_kernel(q, kv, win, packed, flags, choice):
    wf = [win[0, h] for h in range(HEADS)]
    wh = [win[1, h] for h in range(HEADS)]
    kinds = [(a - a * b, a * b, b - a * b, (1 - a) * (1 - b)) for a, b in zip(wf, wh)]
    lone, two, tall, _ = [sum(kind[i] for kind in kinds) for i in range(4)]
    best, start, end = jnp.int32(len(PLANS) - 1), jnp.int32(0), jnp.int32(HEADS)
    for i in reversed(range(len(PLANS) - 1)):
        nf, nh, both = PLANS[i]
        fits = (lone + two <= nf) & (two + tall <= nh) & (two <= both)
        fits = fits & (lone + two + tall <= nf + nh - both)
        best = jnp.where(fits, i, best)
        start = jnp.where(fits, nf - both, start)
        end = jnp.where(fits, nf - both + nh, end)
    choice[0] = best
    middle = jnp.maximum(start, lone)
    gap = middle - lone
    after = end - tall - middle - two
    free = [jnp.int32(0), middle, end - 1, jnp.int32(0)]
    ranks = []
    for kind in kinds:
        i = free[3]
        rest = jnp.where(i < gap, lone + i, jnp.where(i < gap + after, middle + two - gap + i, end - gap - after + i))
        ranks.append(kind[0] * free[0] + kind[1] * free[1] + kind[2] * free[2] + kind[3] * rest)
        free = [free[0] + kind[0], free[1] + kind[1], free[2] - kind[2], free[3] + kind[3]]
    heads = [sum(jnp.where(ranks[h] == s, h, 0) for h in range(HEADS)) for s in range(HEADS)]
    for s in range(HEADS):
        for i in range(3):
            flags[s, i] = win[i, heads[s]]
        flags[s, 3] = ranks[s] % 2 * HALF + ranks[s] // 2
        columns = pl.ds(pl.multiple_of(heads[s] * HD, HD), HD)
        at = s % 2 * HALF + s // 2
        packed[0, at] = kv[0, :, columns]
        packed[1, at] = kv[1, :, columns].T
        packed[2, at] = q[:, columns]


def place_kernel(o, flags, out):
    for h in range(HEADS):
        out[:, h * HD : (h + 1) * HD] = o[flags[h, 3]]


def kernel(
    cfg,
    n_frame,
    n_chip_y,
    packed,
    flags,
    out,
    kv,
    qa,
    acc,
    top,
    rs,
    rr,
    oh,
    own_l,
    own_s,
    own_r,
    z_s,
    z_r,
    q_s,
    q_r,
    ret_s,
    ret_r,
    o_l,
    o_s,
    o_r,
):
    nf, nh, both = cfg
    h0 = nf - both
    h1 = h0 + nh

    def part(start, end, g):
        return (start + 1 - g) // 2, (end + 1 - g) // 2

    f = lax.axis_index("frame")
    height = lax.axis_index("height")
    y = height // 2
    c = height % 2
    other = 1 - c
    z_ok = (f > 0, f < n_frame - 1)
    y_ok = (y > 0, y < n_chip_y - 1)
    z_dev = (f - 1, f + 1)
    y_dev = (y - 1, y + 1)
    partner = {"height": 2 * y + other}

    barrier = pltpu.get_barrier_semaphore()
    pl.semaphore_signal(barrier, inc=1, device_id=partner, device_id_type=MESH)
    for d in range(2):

        @pl.when(z_ok[d])
        def _():
            for g in range(2):
                pl.semaphore_signal(
                    barrier,
                    inc=1,
                    device_id={"frame": z_dev[d], "height": 2 * y + g},
                    device_id_type=MESH,
                )

        @pl.when(y_ok[d])
        def _():
            for g in range(2):
                pl.semaphore_signal(
                    barrier,
                    inc=1,
                    device_id={"height": 2 * y_dev[d] + g},
                    device_id_type=MESH,
                )

    own_loads = (
        pltpu.make_async_copy(
            packed.at[pl.ds(0, 2), pl.ds(c * HALF, HALF)], kv.at[1, :, :, c], own_l.at[0]
        ),
        pltpu.make_async_copy(packed.at[2, pl.ds(c * HALF, HALF)], qa.at[:, 0, c], own_l.at[1]),
    )

    def remote(src, dst, send_sem, recv_sem, device):
        return pltpu.make_async_remote_copy(
            src_ref=src,
            dst_ref=dst,
            send_sem=send_sem,
            recv_sem=recv_sem,
            device_id=device,
            device_id_type=MESH,
        )

    own_copies = (
        remote(
            packed.at[pl.ds(0, 2), pl.ds(other * HALF, HALF)],
            kv.at[1, :, :, c],
            own_s.at[0],
            own_r.at[0],
            partner,
        ),
        remote(
            packed.at[2, pl.ds(other * HALF, HALF)],
            qa.at[:, 0, c],
            own_s.at[1],
            own_r.at[1],
            partner,
        ),
    )

    def z_copy(d, s):
        j, g = s // 2, s % 2
        return remote(
            packed.at[pl.ds(0, 2), g * HALF + j],
            kv.at[2 - 2 * d, :, j, c],
            z_s.at[d],
            z_r.at[1 - d, j],
            {"frame": z_dev[d], "height": 2 * y + g},
        )

    def z_arrival(d, j):
        dst = kv.at[2 * d, :, j]
        return remote(dst, dst, z_s.at[d], z_r.at[d, j], partner)

    def z_sent(d):
        src = packed.at[pl.ds(0, 2), pl.ds(0, nf)]
        return remote(src, src, z_s.at[d], z_r.at[d, 0], partner)

    runs = ((nf, h1), (h0, nf))

    def q_copy(d, i, g):
        j, end = part(*runs[i], g)
        return remote(
            packed.at[2, pl.ds(g * HALF + j, end - j)],
            qa.at[pl.ds(j, end - j), 2 - d, c],
            q_s.at[d],
            q_r.at[1 - d, i],
            {"height": 2 * y_dev[d] + g},
        )

    def q_arrival(d, i, g):
        j, end = part(*runs[i], g)
        dst = qa.at[pl.ds(j, end - j), 1 + d]
        return remote(dst, dst, q_s.at[d], q_r.at[d, i], partner)

    def q_sent(d):
        src = packed.at[2, pl.ds(0, nh)]
        return remote(src, src, q_s.at[d], q_r.at[d, 0], partner)

    def filled(i, g):
        j, end = part(*runs[i], g)
        return j < end

    def ret_copy(d, j):
        return remote(
            rs.at[d, j],
            rr.at[1 - d, j],
            ret_s.at[d, j],
            ret_r.at[1 - d, j],
            {"height": 2 * y_dev[d] + c},
        )

    def o_copy(j):
        return remote(oh.at[other, j], out.at[c * HALF + j], o_s, o_r, partner)

    def o_arrivals():
        return remote(oh.at[other], out.at[pl.ds(other * HALF, HALF)], o_s, o_r, partner)

    def o_store(j):
        return pltpu.make_async_copy(oh.at[c, j], out.at[c * HALF + j], o_l)

    def o_stores():
        return pltpu.make_async_copy(oh.at[c], out.at[pl.ds(c * HALF, HALF)], o_l)

    for copy in own_loads:
        copy.start()

    for d in range(2):

        @pl.when(jnp.logical_not(y_ok[d]))
        def _():
            rr[d] = jnp.zeros(rr.shape[1:], rr.dtype)

        @pl.when(jnp.logical_not(z_ok[d]))
        def _():
            kv[2 * d] = jnp.zeros(kv.shape[1:], kv.dtype)

    pl.semaphore_wait(
        barrier,
        1
        + 2 * sum(jnp.where(ok, 1, 0) for ok in z_ok)
        + 2 * sum(jnp.where(ok, 1, 0) for ok in y_ok),
    )

    def send_z(slots):
        for d in range(2):

            @pl.when(z_ok[d])
            def _():
                for s in slots:
                    z_copy(d, s).start()

    for copy in own_copies:
        copy.start()

    batches = [[s for s in (2 * j + 1, 2 * j) if s < nf] for j in reversed(range((nf + 1) // 2))]
    window = 2 + nf % 2
    for slots in batches[:window]:
        send_z(slots)
    for i in range(2):
        for d in range(2):

            @pl.when(y_ok[d])
            def _():
                for g in range(2):
                    if filled(i, g):
                        q_copy(d, i, g).start()

    key_side = lax.broadcasted_iota(jnp.int32, (W, 3 * CHIP), 0) // TW
    query_side = lax.broadcasted_iota(jnp.int32, (W, 3 * CHIP), 1) % W // TW
    apart = jnp.where(key_side == query_side, 0.0, NEG).astype(jnp.float32)
    ones = jnp.ones((EXTRA, CHIP), jnp.bfloat16)

    def shut(j, column):
        return (1 - flags[2 * j + c, column]).astype(jnp.float32)

    def keys(tile, j):
        return kv[tile, 0, j].reshape(CHIP, HD)

    def values(tile, j):
        vt = jnp.concatenate([kv[tile, 1, j, 0], kv[tile, 1, j, 1]], axis=1)
        return jnp.concatenate([vt, ones], axis=0)

    def scores(k, j, parts):
        q = qa[j, 0:parts].reshape(parts * CHIP, HD)
        return dot(k, q, ((1,), (1,)))

    def weights(s, m):
        return jnp.exp2((s - m) * SCALE).astype(jnp.bfloat16)

    def here(j, parts):
        n = parts * CHIP
        s = scores(keys(1, j), j, parts)
        bias = apart[:, :n] * shut(j, 2)
        s = (s.reshape(CHIP // W, W, n) + bias[None]).reshape(CHIP, n)
        m = jnp.max(s, axis=0, keepdims=True)
        top[j, 0:1, 0:n] = m
        acc[j, :, 0:n] = dot(values(1, j), weights(s, m), ((1,), (0,)))

    def wait_z(j):
        for d in range(2):

            @pl.when(z_ok[d])
            def _():
                z_arrival(d, j).wait_recv()

    def around(j, parts):
        n = parts * CHIP
        s = scores(jnp.concatenate([keys(0, j), keys(2, j)], axis=0), j, parts)
        width = apart[:, :n] * shut(j, 2)
        closed = shut(j, 0) * NEG
        bias = jnp.stack([width + jnp.where(z_ok[d], closed, NEG) for d in range(2)])[:, None]
        s = (s.reshape(2, CHIP // W, W, n) + bias).reshape(2 * CHIP, n)
        m_old = top[j, 0:1, 0:n]
        m = jnp.maximum(m_old, jnp.max(s, axis=0, keepdims=True))
        vt = jnp.concatenate([values(0, j), values(2, j)], axis=1)
        fade = jnp.exp2((m_old - m) * SCALE)
        top[j, 0:1, 0:n] = m
        acc[j, :, 0:n] = acc[j, :, 0:n] * fade + dot(vt, weights(s, m), ((1,), (0,)))

    def give_back(j):
        n = slice(CHIP, 3 * CHIP)
        m = top[j, 0:1, n]
        total = acc[j, HD : HD + 1, n]
        o = (acc[j, 0:HD, n] * (1.0 / total)).astype(jnp.bfloat16)
        level = m * SCALE + jnp.log2(total)
        a = level.astype(jnp.bfloat16).astype(jnp.float32)
        b = (level - a).astype(jnp.bfloat16).astype(jnp.float32)
        row = lax.broadcasted_iota(jnp.int32, (EXTRA, 2 * CHIP), 0)
        rest = jnp.where(row == 2, level - a - b, 0.0)
        digits = jnp.where(row == 0, a, jnp.where(row == 1, b, rest)).astype(jnp.bfloat16)
        for d in range(2):
            rs[d, j, 0:HD] = o[:, d * CHIP : (d + 1) * CHIP]
            rs[d, j, HD : HD + EXTRA] = digits[:, d * CHIP : (d + 1) * CHIP]
        for d in range(2):

            @pl.when(y_ok[d])
            def _():
                ret_copy(d, j).start()

    def finish(j, o):
        o = o.T.astype(jnp.bfloat16)
        oh[0, j] = o[:TOK]
        oh[1, j] = o[TOK:]
        o_copy(j).start()
        o_store(j).start()

    def alone(j):
        finish(j, acc[j, 0:HD, 0:CHIP] * (1.0 / acc[j, HD : HD + 1, 0:CHIP]))

    def join(j):
        for d in range(2):

            @pl.when(y_ok[d])
            def _():
                ret_copy(1 - d, j).wait_recv()
                ret_copy(d, j).wait_send()

        m = top[j, 0:1, 0:CHIP] * SCALE
        total = acc[j, HD : HD + 1, 0:CHIP]
        low = shut(j, 1) * NEG
        levels = []
        for d in range(2):
            digits = rr[d, j, HD : HD + EXTRA].astype(jnp.float32)
            level = jnp.sum(digits, axis=0, keepdims=True)
            levels.append(level + jnp.where(y_ok[d], low, NEG))
        best = jnp.maximum(m + jnp.log2(total), jnp.maximum(levels[0], levels[1]))
        w = [jnp.exp2(x - best) for x in (m, *levels)]
        over = 1.0 / (total * w[0] + w[1] + w[2])
        o = acc[j, 0:HD, 0:CHIP] * (w[0] * over)
        for d in range(2):
            o = o + rr[d, j, 0:HD].astype(jnp.float32) * (w[d + 1] * over)
        finish(j, o)

    for copy in own_loads:
        copy.wait()
    for copy in own_copies:
        copy.wait_recv()

    lo, hi = part(h0, h1, c)
    my_z = part(0, nf, c)[1]
    n_in = my_z - lo
    n_out = hi - my_z

    @pl.loop(0, lo + HALF - hi)
    def _(n):
        j = jnp.where(n < lo, n, n - lo + hi)
        here(j, 1)

        @pl.when(j >= hi)
        def _():
            alone(j)

    @pl.loop(0, n_out + n_in)
    def _(n):
        j = jnp.where(n < n_out, my_z + n, my_z - 1 - (n - n_out))
        for i in range(2):
            for d in range(2):
                for g in range(2):
                    if filled(i, g):

                        @pl.when((n == (n_out if i else 0)) & (c == g) & y_ok[d])
                        def _():
                            q_arrival(d, i, g).wait_recv()

        here(j, 3)

        @pl.when(n < n_out)
        def _():
            give_back(j)

    @pl.loop(my_z, hi)
    def _(j):
        join(j)

    @pl.loop(0, n_in)
    def _(n):
        j = my_z - 1 - n
        wait_z(j)
        for i, slots in enumerate(batches[window:]):

            @pl.when(n == i)
            def _():
                send_z(slots)

        around(j, 3)
        give_back(j)

    for i, slots in enumerate(batches[window:]):

        @pl.when(n_in <= i)
        def _():
            send_z(slots)

    @pl.loop(0, n_in)
    def _(n):
        join(my_z - 1 - n)

    if h0 > 0:

        @pl.loop(0, lo)
        def _(i):
            j = lo - 1 - i
            wait_z(j)
            around(j, 1)
            alone(j)

    for copy in own_copies:
        copy.wait_send()
    for d in range(2):

        @pl.when(z_ok[d])
        def _():
            z_sent(d).wait_send()

        @pl.when(y_ok[d])
        def _():
            q_sent(d).wait_send()

    o_stores().wait()
    o_arrivals().wait()


def attend(index, n_frame, n_chip_y, packed, flags):
    nf, nh, both = PLANS[index]
    assert both <= min(nf, nh) and nf + nh - both <= HEADS
    bf16, f32 = jnp.bfloat16, jnp.float32
    dma = pltpu.SemaphoreType.DMA
    return pl.pallas_call(
        functools.partial(kernel, PLANS[index], n_frame, n_chip_y),
        out_shape=jax.ShapeDtypeStruct((HEADS, TOK, HD), bf16),
        in_specs=[pl.BlockSpec(memory_space=pl.ANY), pl.BlockSpec(memory_space=pltpu.SMEM)],
        out_specs=pl.BlockSpec(memory_space=pl.ANY),
        scratch_shapes=[
            pltpu.VMEM((3, 2, HALF, 2, TOK, HD), bf16),
            pltpu.VMEM((HALF, 3, 2, TOK, HD), bf16),
            pltpu.VMEM((HALF, HD + EXTRA, 3 * CHIP), f32),
            pltpu.VMEM((HALF, 8, 3 * CHIP), f32),
            pltpu.VMEM((2, HALF, HD + EXTRA, CHIP), bf16),
            pltpu.VMEM((2, HALF, HD + EXTRA, CHIP), bf16),
            pltpu.VMEM((2, HALF, TOK, HD), bf16),
            dma((2,)),
            dma((2,)),
            dma((2,)),
            dma((2,)),
            dma((2, HALF)),
            dma((2,)),
            dma((2, 2)),
            dma((2, HALF)),
            dma((2, HALF)),
            dma,
            dma,
            dma,
        ],
        compiler_params=pltpu.CompilerParams(
            collective_id=index,
            has_side_effects=True,
            vmem_limit_bytes=32 * 1024 * 1024,
        ),
    )(packed, flags)


def shards(queries, key_value, windows):
    n_frame = lax.axis_size("frame")
    n_chip_y = lax.axis_size("height") // 2
    width = HEADS * HD
    vmem = pl.BlockSpec(memory_space=pltpu.VMEM)
    smem = pl.BlockSpec(memory_space=pltpu.SMEM)
    packed, flags, choice = pl.pallas_call(
        sort_kernel,
        out_shape=(
            jax.ShapeDtypeStruct((3, HEADS, TOK, HD), jnp.bfloat16),
            jax.ShapeDtypeStruct((HEADS, 4), jnp.int32),
            jax.ShapeDtypeStruct((1,), jnp.int32),
        ),
        in_specs=[vmem, vmem, smem],
        out_specs=(vmem, smem, smem),
    )(queries.reshape(TOK, width), key_value.reshape(2, TOK, width), windows.T)
    branches = [functools.partial(attend, i, n_frame, n_chip_y) for i in range(len(PLANS))]
    slots = lax.switch(choice[0], branches, packed, flags)
    result = pl.pallas_call(
        place_kernel,
        out_shape=jax.ShapeDtypeStruct((TOK, width), jnp.bfloat16),
        in_specs=[vmem, smem],
        out_specs=vmem,
    )(slots, flags)
    return result.reshape(queries.shape)


def solution(mesh):
    in_specs = (
        P(("cand", "frame"), "height", None, None),
        P(None, ("cand", "frame"), "height", None, None),
        P(),
    )
    out_specs = P(("cand", "frame"), "height", None, None)
    return jax.shard_map(shards, mesh=mesh, in_specs=in_specs, out_specs=out_specs, check_vma=False)
```

```python
import functools
import math

import jax
import jax.numpy as jnp
from jax import lax
from jax.experimental import pallas as pl
from jax.experimental.pallas import tpu as pltpu
from jax.sharding import PartitionSpec as P

HEADS = 12
HALF = HEADS // 2
HD = 128
TOK = 128
CHIP = 2 * TOK
W = 16
TW = 8
NEG = -1e30
EXTRA = 16
SCALE = math.log2(math.e) / math.sqrt(HD)
RUN = 4
MESH = pl.DeviceIdType.MESH


def dot(a, b, dims):
    return lax.dot_general(a, b, ((dims[0], dims[1]), ((), ())), preferred_element_type=jnp.float32)


PLANS = (
    (4, 5, 2),
    (5, 6, 3),
    (5, 7, 2),
    (6, 7, 4),
    (6, 8, 3),
    (7, 8, 5),
    (7, 9, 4),
    (8, 9, 6),
    (9, 10, 7),
    (12, 12, 12),
)


def sort_kernel(q, kv, win, packed, flags, choice):
    wf = [win[0, h] for h in range(HEADS)]
    wh = [win[1, h] for h in range(HEADS)]
    kinds = [(a - a * b, a * b, b - a * b, (1 - a) * (1 - b)) for a, b in zip(wf, wh)]
    lone, two, tall, _ = [sum(kind[i] for kind in kinds) for i in range(4)]
    best, start, end = jnp.int32(len(PLANS) - 1), jnp.int32(0), jnp.int32(HEADS)
    for i in reversed(range(len(PLANS) - 1)):
        nf, nh, both = PLANS[i]
        fits = (lone + two <= nf) & (two + tall <= nh) & (two <= both)
        fits = fits & (lone + two + tall <= nf + nh - both)
        best = jnp.where(fits, i, best)
        start = jnp.where(fits, nf - both, start)
        end = jnp.where(fits, nf - both + nh, end)
    choice[0] = best
    middle = jnp.maximum(start, lone)
    gap = middle - lone
    after = end - tall - middle - two
    free = [jnp.int32(0), middle, end - 1, jnp.int32(0)]
    ranks = []
    for kind in kinds:
        i = free[3]
        rest = jnp.where(i < gap, lone + i, jnp.where(i < gap + after, middle + two - gap + i, end - gap - after + i))
        ranks.append(kind[0] * free[0] + kind[1] * free[1] + kind[2] * free[2] + kind[3] * rest)
        free = [free[0] + kind[0], free[1] + kind[1], free[2] - kind[2], free[3] + kind[3]]
    heads = [sum(jnp.where(ranks[h] == s, h, 0) for h in range(HEADS)) for s in range(HEADS)]
    for s in range(HEADS):
        for i in range(3):
            flags[s, i] = win[i, heads[s]]
        flags[s, 3] = ranks[s] % 2 * HALF + ranks[s] // 2
        columns = pl.ds(pl.multiple_of(heads[s] * HD, HD), HD)
        at = s % 2 * HALF + s // 2
        packed[0, at] = kv[0, :, columns]
        packed[1, at] = kv[1, :, columns].T
        packed[2, at] = q[:, columns]


def place_kernel(o, flags, out):
    for h in range(HEADS):
        out[:, h * HD : (h + 1) * HD] = o[flags[h, 3]]


def kernel(
    cfg,
    n_frame,
    n_chip_y,
    packed,
    flags,
    out,
    kv,
    qa,
    acc,
    top,
    rs,
    rr,
    oh,
    own_l,
    own_s,
    own_r,
    z_s,
    z_r,
    q_s,
    q_r,
    ret_s,
    ret_r,
    o_l,
    o_s,
    o_r,
):
    nf, nh, both = cfg
    h0 = nf - both
    h1 = h0 + nh

    def part(start, end, g):
        return (start + 1 - g) // 2, (end + 1 - g) // 2

    f = lax.axis_index("frame")
    height = lax.axis_index("height")
    y = height // 2
    c = height % 2
    other = 1 - c
    z_ok = (f > 0, f < n_frame - 1)
    y_ok = (y > 0, y < n_chip_y - 1)
    far = jnp.where(f % RUN == 0, 0, 1)
    near = 1 - far
    crosses = (f % RUN == 0) | (f % RUN == RUN - 1)

    def has_z(d):
        return (f - 1 + 2 * d >= 0) & (f - 1 + 2 * d < n_frame)

    y_dev = (y - 1, y + 1)
    partner = {"height": 2 * y + other}

    barrier = pltpu.get_barrier_semaphore()
    pl.semaphore_signal(barrier, inc=1, device_id=partner, device_id_type=MESH)
    for d in range(2):

        @pl.when(z_ok[d])
        def _():
            for g in range(2):
                pl.semaphore_signal(
                    barrier,
                    inc=1,
                    device_id={"frame": f - 1 + 2 * d, "height": 2 * y + g},
                    device_id_type=MESH,
                )

        @pl.when(y_ok[d])
        def _():
            for g in range(2):
                pl.semaphore_signal(
                    barrier,
                    inc=1,
                    device_id={"height": 2 * y_dev[d] + g},
                    device_id_type=MESH,
                )

    own_loads = (
        pltpu.make_async_copy(
            packed.at[pl.ds(0, 2), pl.ds(c * HALF, HALF)], kv.at[1, :, :, c], own_l.at[0]
        ),
        pltpu.make_async_copy(packed.at[2, pl.ds(c * HALF, HALF)], qa.at[:, 0, c], own_l.at[1]),
    )

    def remote(src, dst, send_sem, recv_sem, device):
        return pltpu.make_async_remote_copy(
            src_ref=src,
            dst_ref=dst,
            send_sem=send_sem,
            recv_sem=recv_sem,
            device_id=device,
            device_id_type=MESH,
        )

    own_copies = (
        remote(
            packed.at[pl.ds(0, 2), pl.ds(other * HALF, HALF)],
            kv.at[1, :, :, c],
            own_s.at[0],
            own_r.at[0],
            partner,
        ),
        remote(
            packed.at[2, pl.ds(other * HALF, HALF)],
            qa.at[:, 0, c],
            own_s.at[1],
            own_r.at[1],
            partner,
        ),
    )

    def z_copy(d, s):
        j, g = s // 2, s % 2
        return remote(
            packed.at[pl.ds(0, 2), g * HALF + j],
            kv.at[2 - 2 * d, :, j, c],
            z_s.at[d],
            z_r.at[1 - d, j],
            {"frame": f - 1 + 2 * d, "height": 2 * y + g},
        )

    def z_arrival(d, j):
        dst = kv.at[2 * d, :, j]
        return remote(dst, dst, z_s.at[d], z_r.at[d, j], partner)

    def z_sent(d):
        src = packed.at[pl.ds(0, 2), pl.ds(0, nf)]
        return remote(src, src, z_s.at[d], z_r.at[d, 0], partner)

    runs = ((nf, h1), (h0, nf))

    def q_copy(d, i, g):
        j, end = part(*runs[i], g)
        return remote(
            packed.at[2, pl.ds(g * HALF + j, end - j)],
            qa.at[pl.ds(j, end - j), 2 - d, c],
            q_s.at[d],
            q_r.at[1 - d, i],
            {"height": 2 * y_dev[d] + g},
        )

    def q_arrival(d, i, g):
        j, end = part(*runs[i], g)
        dst = qa.at[pl.ds(j, end - j), 1 + d]
        return remote(dst, dst, q_s.at[d], q_r.at[d, i], partner)

    def q_sent(d):
        src = packed.at[2, pl.ds(0, nh)]
        return remote(src, src, q_s.at[d], q_r.at[d, 0], partner)

    def filled(i, g):
        j, end = part(*runs[i], g)
        return j < end

    def ret_copy(d, j):
        return remote(
            rs.at[d, j],
            rr.at[1 - d, j],
            ret_s.at[d, j],
            ret_r.at[1 - d, j],
            {"height": 2 * y_dev[d] + c},
        )

    def o_copy(j):
        return remote(oh.at[other, j], out.at[c * HALF + j], o_s, o_r, partner)

    def o_arrivals():
        return remote(oh.at[other], out.at[pl.ds(other * HALF, HALF)], o_s, o_r, partner)

    def o_store(j):
        return pltpu.make_async_copy(oh.at[c, j], out.at[c * HALF + j], o_l)

    def o_stores():
        return pltpu.make_async_copy(oh.at[c], out.at[pl.ds(c * HALF, HALF)], o_l)

    for copy in own_loads:
        copy.start()

    for d in range(2):

        @pl.when(jnp.logical_not(y_ok[d]))
        def _():
            rr[d] = jnp.zeros(rr.shape[1:], rr.dtype)

        @pl.when(jnp.logical_not(z_ok[d]))
        def _():
            kv[2 * d] = jnp.zeros(kv.shape[1:], kv.dtype)

    pl.semaphore_wait(
        barrier,
        1
        + 2 * sum(jnp.where(ok, 1, 0) for ok in z_ok)
        + 2 * sum(jnp.where(ok, 1, 0) for ok in y_ok),
    )

    batches = [[s for s in (2 * j + 1, 2 * j) if s < nf] for j in reversed(range((nf + 1) // 2))]
    window = 2

    def send_z(d, chosen):
        for slots in chosen:
            for s in slots:
                z_copy(d, s).start()

    @pl.when(has_z(far))
    def _():
        send_z(far, batches[:window])

    @pl.when(has_z(far) & crosses)
    def _():
        send_z(far, batches[window:])

    for copy in own_copies:
        copy.start()

    @pl.when(has_z(near))
    def _():
        send_z(near, batches[:window])

    for i in range(2):
        for d in range(2):

            @pl.when(y_ok[d])
            def _():
                for g in range(2):
                    if filled(i, g):
                        q_copy(d, i, g).start()

    key_side = lax.broadcasted_iota(jnp.int32, (W, 3 * CHIP), 0) // TW
    query_side = lax.broadcasted_iota(jnp.int32, (W, 3 * CHIP), 1) % W // TW
    apart = jnp.where(key_side == query_side, 0.0, NEG).astype(jnp.float32)
    ones = jnp.ones((EXTRA, CHIP), jnp.bfloat16)

    def shut(j, column):
        return (1 - flags[2 * j + c, column]).astype(jnp.float32)

    def keys(tile, j):
        return kv[tile, 0, j].reshape(CHIP, HD)

    def values(tile, j):
        vt = jnp.concatenate([kv[tile, 1, j, 0], kv[tile, 1, j, 1]], axis=1)
        return jnp.concatenate([vt, ones], axis=0)

    def scores(k, j, parts):
        q = qa[j, 0:parts].reshape(parts * CHIP, HD)
        return dot(k, q, ((1,), (1,)))

    def weights(s, m):
        return jnp.exp2((s - m) * SCALE).astype(jnp.bfloat16)

    def here(j, parts):
        n = parts * CHIP
        s = scores(keys(1, j), j, parts)
        bias = apart[:, :n] * shut(j, 2)
        s = (s.reshape(CHIP // W, W, n) + bias[None]).reshape(CHIP, n)
        m = jnp.max(s, axis=0, keepdims=True)
        top[j, 0:1, 0:n] = m
        acc[j, :, 0:n] = dot(values(1, j), weights(s, m), ((1,), (0,)))

    def wait_z(d, j):
        @pl.when(has_z(d))
        def _():
            z_arrival(d, j).wait_recv()

    def around(j, parts):
        n = parts * CHIP
        s = scores(jnp.concatenate([keys(0, j), keys(2, j)], axis=0), j, parts)
        width = apart[:, :n] * shut(j, 2)
        closed = shut(j, 0) * NEG
        bias = jnp.stack([width + jnp.where(z_ok[d], closed, NEG) for d in range(2)])[:, None]
        s = (s.reshape(2, CHIP // W, W, n) + bias).reshape(2 * CHIP, n)
        m_old = top[j, 0:1, 0:n]
        m = jnp.maximum(m_old, jnp.max(s, axis=0, keepdims=True))
        vt = jnp.concatenate([values(0, j), values(2, j)], axis=1)
        fade = jnp.exp2((m_old - m) * SCALE)
        top[j, 0:1, 0:n] = m
        acc[j, :, 0:n] = acc[j, :, 0:n] * fade + dot(vt, weights(s, m), ((1,), (0,)))

    def give_back(j):
        n = slice(CHIP, 3 * CHIP)
        m = top[j, 0:1, n]
        total = acc[j, HD : HD + 1, n]
        o = (acc[j, 0:HD, n] * (1.0 / total)).astype(jnp.bfloat16)
        level = m * SCALE + jnp.log2(total)
        a = level.astype(jnp.bfloat16).astype(jnp.float32)
        b = (level - a).astype(jnp.bfloat16).astype(jnp.float32)
        row = lax.broadcasted_iota(jnp.int32, (EXTRA, 2 * CHIP), 0)
        rest = jnp.where(row == 2, level - a - b, 0.0)
        digits = jnp.where(row == 0, a, jnp.where(row == 1, b, rest)).astype(jnp.bfloat16)
        for d in range(2):
            rs[d, j, 0:HD] = o[:, d * CHIP : (d + 1) * CHIP]
            rs[d, j, HD : HD + EXTRA] = digits[:, d * CHIP : (d + 1) * CHIP]
        for d in range(2):

            @pl.when(y_ok[d])
            def _():
                ret_copy(d, j).start()

    def finish(j, o):
        o = o.T.astype(jnp.bfloat16)
        oh[0, j] = o[:TOK]
        oh[1, j] = o[TOK:]
        o_copy(j).start()
        o_store(j).start()

    def alone(j):
        finish(j, acc[j, 0:HD, 0:CHIP] * (1.0 / acc[j, HD : HD + 1, 0:CHIP]))

    def join(j):
        for d in range(2):

            @pl.when(y_ok[d])
            def _():
                ret_copy(1 - d, j).wait_recv()
                ret_copy(d, j).wait_send()

        m = top[j, 0:1, 0:CHIP] * SCALE
        total = acc[j, HD : HD + 1, 0:CHIP]
        low = shut(j, 1) * NEG
        levels = []
        for d in range(2):
            digits = rr[d, j, HD : HD + EXTRA].astype(jnp.float32)
            level = jnp.sum(digits, axis=0, keepdims=True)
            levels.append(level + jnp.where(y_ok[d], low, NEG))
        best = jnp.maximum(m + jnp.log2(total), jnp.maximum(levels[0], levels[1]))
        w = [jnp.exp2(x - best) for x in (m, *levels)]
        over = 1.0 / (total * w[0] + w[1] + w[2])
        o = acc[j, 0:HD, 0:CHIP] * (w[0] * over)
        for d in range(2):
            o = o + rr[d, j, 0:HD].astype(jnp.float32) * (w[d + 1] * over)
        finish(j, o)

    for copy in own_loads:
        copy.wait()
    for copy in own_copies:
        copy.wait_recv()

    lo, hi = part(h0, h1, c)
    my_z = part(0, nf, c)[1]
    n_in = my_z - lo
    n_out = hi - my_z

    @pl.loop(0, lo + HALF - hi)
    def _(n):
        j = jnp.where(n < lo, n, n - lo + hi)
        here(j, 1)

        @pl.when(j >= hi)
        def _():
            alone(j)

    @pl.loop(0, n_out + n_in)
    def _(n):
        j = jnp.where(n < n_out, my_z + n, my_z - 1 - (n - n_out))
        for i in range(2):
            for d in range(2):
                for g in range(2):
                    if filled(i, g):

                        @pl.when((n == (n_out if i else 0)) & (c == g) & y_ok[d])
                        def _():
                            q_arrival(d, i, g).wait_recv()

        here(j, 3)

        @pl.when(n < n_out)
        def _():
            give_back(j)

    @pl.loop(my_z, hi)
    def _(j):
        join(j)

    @pl.loop(0, n_in)
    def _(n):
        j = my_z - 1 - n
        for d in (near, far):
            wait_z(d, j)
            later = has_z(d) if d is near else has_z(d) & jnp.logical_not(crosses)
            for i in range(len(batches) - window):

                @pl.when((n == i) & later)
                def _():
                    send_z(d, batches[window + i : window + i + 1])

        around(j, 3)
        give_back(j)

    for i in range(len(batches) - window):
        for d in (near, far):
            later = has_z(d) if d is near else has_z(d) & jnp.logical_not(crosses)

            @pl.when((n_in <= i) & later)
            def _():
                send_z(d, batches[window + i : window + i + 1])

    @pl.loop(0, n_in)
    def _(n):
        join(my_z - 1 - n)

    if h0 > 0:

        @pl.loop(0, lo)
        def _(i):
            j = lo - 1 - i
            wait_z(near, j)
            wait_z(far, j)
            around(j, 1)
            alone(j)

    for copy in own_copies:
        copy.wait_send()
    for d in range(2):

        @pl.when(z_ok[d])
        def _():
            z_sent(d).wait_send()

        @pl.when(y_ok[d])
        def _():
            q_sent(d).wait_send()

    o_stores().wait()
    o_arrivals().wait()


def attend(index, n_frame, n_chip_y, packed, flags):
    nf, nh, both = PLANS[index]
    assert both <= min(nf, nh) and nf + nh - both <= HEADS
    bf16, f32 = jnp.bfloat16, jnp.float32
    dma = pltpu.SemaphoreType.DMA
    return pl.pallas_call(
        functools.partial(kernel, PLANS[index], n_frame, n_chip_y),
        out_shape=jax.ShapeDtypeStruct((HEADS, TOK, HD), bf16),
        in_specs=[pl.BlockSpec(memory_space=pl.ANY), pl.BlockSpec(memory_space=pltpu.SMEM)],
        out_specs=pl.BlockSpec(memory_space=pl.ANY),
        scratch_shapes=[
            pltpu.VMEM((3, 2, HALF, 2, TOK, HD), bf16),
            pltpu.VMEM((HALF, 3, 2, TOK, HD), bf16),
            pltpu.VMEM((HALF, HD + EXTRA, 3 * CHIP), f32),
            pltpu.VMEM((HALF, 8, 3 * CHIP), f32),
            pltpu.VMEM((2, HALF, HD + EXTRA, CHIP), bf16),
            pltpu.VMEM((2, HALF, HD + EXTRA, CHIP), bf16),
            pltpu.VMEM((2, HALF, TOK, HD), bf16),
            dma((2,)),
            dma((2,)),
            dma((2,)),
            dma((2,)),
            dma((2, HALF)),
            dma((2,)),
            dma((2, 2)),
            dma((2, HALF)),
            dma((2, HALF)),
            dma,
            dma,
            dma,
        ],
        compiler_params=pltpu.CompilerParams(
            collective_id=index,
            has_side_effects=True,
            vmem_limit_bytes=32 * 1024 * 1024,
        ),
    )(packed, flags)


def shards(queries, key_value, windows):
    n_frame = lax.axis_size("frame")
    n_chip_y = lax.axis_size("height") // 2
    width = HEADS * HD
    vmem = pl.BlockSpec(memory_space=pltpu.VMEM)
    smem = pl.BlockSpec(memory_space=pltpu.SMEM)
    packed, flags, choice = pl.pallas_call(
        sort_kernel,
        out_shape=(
            jax.ShapeDtypeStruct((3, HEADS, TOK, HD), jnp.bfloat16),
            jax.ShapeDtypeStruct((HEADS, 4), jnp.int32),
            jax.ShapeDtypeStruct((1,), jnp.int32),
        ),
        in_specs=[vmem, vmem, smem],
        out_specs=(vmem, smem, smem),
    )(queries.reshape(TOK, width), key_value.reshape(2, TOK, width), windows.T)
    branches = [functools.partial(attend, i, n_frame, n_chip_y) for i in range(len(PLANS))]
    slots = lax.switch(choice[0], branches, packed, flags)
    result = pl.pallas_call(
        place_kernel,
        out_shape=jax.ShapeDtypeStruct((TOK, width), jnp.bfloat16),
        in_specs=[vmem, smem],
        out_specs=vmem,
    )(slots, flags)
    return result.reshape(queries.shape)


def solution(mesh):
    in_specs = (
        P(("cand", "frame"), "height", None, None),
        P(None, ("cand", "frame"), "height", None, None),
        P(),
    )
    out_specs = P(("cand", "frame"), "height", None, None)
    return jax.shard_map(shards, mesh=mesh, in_specs=in_specs, out_specs=out_specs, check_vma=False)
```

```python
import functools
import math

import jax
import jax.numpy as jnp
from jax import lax
from jax.experimental import pallas as pl
from jax.experimental.pallas import tpu as pltpu
from jax.sharding import PartitionSpec as P

HEADS = 12
HALF = HEADS // 2
HD = 128
TOK = 128
CHIP = 2 * TOK
W = 16
TW = 8
NEG = -1e30
EXTRA = 16
SCALE = math.log2(math.e) / math.sqrt(HD)
RUN = 4
MESH = pl.DeviceIdType.MESH


def dot(a, b, dims):
    return lax.dot_general(a, b, ((dims[0], dims[1]), ((), ())), preferred_element_type=jnp.float32)


PLANS = (
    (4, 5, 2),
    (5, 6, 3),
    (5, 7, 2),
    (6, 7, 4),
    (6, 8, 3),
    (7, 8, 5),
    (7, 9, 4),
    (8, 9, 6),
    (9, 10, 7),
    (12, 12, 12),
)


def sort_kernel(q, kv, win, packed, flags, choice):
    wf = [win[0, h] for h in range(HEADS)]
    wh = [win[1, h] for h in range(HEADS)]
    kinds = [(a - a * b, a * b, b - a * b, (1 - a) * (1 - b)) for a, b in zip(wf, wh)]
    lone, two, tall, _ = [sum(kind[i] for kind in kinds) for i in range(4)]
    best, start, end = jnp.int32(len(PLANS) - 1), jnp.int32(0), jnp.int32(HEADS)
    for i in reversed(range(len(PLANS) - 1)):
        nf, nh, both = PLANS[i]
        fits = (lone + two <= nf) & (two + tall <= nh) & (two <= both)
        fits = fits & (lone + two + tall <= nf + nh - both)
        best = jnp.where(fits, i, best)
        start = jnp.where(fits, nf - both, start)
        end = jnp.where(fits, nf - both + nh, end)
    choice[0] = best
    middle = jnp.maximum(start, lone)
    gap = middle - lone
    after = end - tall - middle - two
    free = [jnp.int32(0), middle, end - 1, jnp.int32(0)]
    ranks = []
    for kind in kinds:
        i = free[3]
        rest = jnp.where(i < gap, lone + i, jnp.where(i < gap + after, middle + two - gap + i, end - gap - after + i))
        ranks.append(kind[0] * free[0] + kind[1] * free[1] + kind[2] * free[2] + kind[3] * rest)
        free = [free[0] + kind[0], free[1] + kind[1], free[2] - kind[2], free[3] + kind[3]]
    heads = [sum(jnp.where(ranks[h] == s, h, 0) for h in range(HEADS)) for s in range(HEADS)]
    for s in range(HEADS):
        for i in range(3):
            flags[s, i] = win[i, heads[s]]
        flags[s, 3] = ranks[s] % 2 * HALF + ranks[s] // 2
        columns = pl.ds(pl.multiple_of(heads[s] * HD, HD), HD)
        at = s % 2 * HALF + s // 2
        packed[0, at] = kv[0, :, columns]
        packed[1, at] = kv[1, :, columns].T
        packed[2, at] = q[:, columns]


def place_kernel(o, flags, out):
    for h in range(HEADS):
        out[:, h * HD : (h + 1) * HD] = o[flags[h, 3]]


def kernel(
    cfg,
    n_frame,
    n_chip_y,
    packed,
    flags,
    out,
    kv,
    qa,
    acc,
    top,
    rs,
    rr,
    oh,
    own_l,
    own_s,
    own_r,
    z_s,
    z_r,
    q_s,
    q_r,
    ret_s,
    ret_r,
    o_l,
    o_s,
    o_r,
):
    nf, nh, both = cfg
    h0 = nf - both
    h1 = h0 + nh

    def part(start, end, g):
        return (start + 1 - g) // 2, (end + 1 - g) // 2

    f = lax.axis_index("frame")
    height = lax.axis_index("height")
    y = height // 2
    c = height % 2
    other = 1 - c
    z_ok = (f > 0, f < n_frame - 1)
    y_ok = (y > 0, y < n_chip_y - 1)
    far = jnp.where(f % RUN == 0, 0, 1)
    near = 1 - far
    crosses = (f % RUN == 0) | (f % RUN == RUN - 1)

    def has_z(d):
        return (f - 1 + 2 * d >= 0) & (f - 1 + 2 * d < n_frame)

    y_dev = (y - 1, y + 1)
    partner = {"height": 2 * y + other}

    barrier = pltpu.get_barrier_semaphore()
    pl.semaphore_signal(barrier, inc=1, device_id=partner, device_id_type=MESH)
    for d in range(2):

        @pl.when(z_ok[d])
        def _():
            for g in range(2):
                pl.semaphore_signal(
                    barrier,
                    inc=1,
                    device_id={"frame": f - 1 + 2 * d, "height": 2 * y + g},
                    device_id_type=MESH,
                )

        @pl.when(y_ok[d])
        def _():
            for g in range(2):
                pl.semaphore_signal(
                    barrier,
                    inc=1,
                    device_id={"height": 2 * y_dev[d] + g},
                    device_id_type=MESH,
                )

    own_loads = (
        pltpu.make_async_copy(
            packed.at[pl.ds(0, 2), pl.ds(c * HALF, HALF)], kv.at[1, :, :, c], own_l.at[0]
        ),
        pltpu.make_async_copy(packed.at[2, pl.ds(c * HALF, HALF)], qa.at[:, 0, c], own_l.at[1]),
    )

    def remote(src, dst, send_sem, recv_sem, device):
        return pltpu.make_async_remote_copy(
            src_ref=src,
            dst_ref=dst,
            send_sem=send_sem,
            recv_sem=recv_sem,
            device_id=device,
            device_id_type=MESH,
        )

    own_copies = (
        remote(
            packed.at[pl.ds(0, 2), pl.ds(other * HALF, HALF)],
            kv.at[1, :, :, c],
            own_s.at[0],
            own_r.at[0],
            partner,
        ),
        remote(
            packed.at[2, pl.ds(other * HALF, HALF)],
            qa.at[:, 0, c],
            own_s.at[1],
            own_r.at[1],
            partner,
        ),
    )

    def z_copy(d, s):
        j, g = s // 2, s % 2
        return remote(
            packed.at[pl.ds(0, 2), g * HALF + j],
            kv.at[2 - 2 * d, :, j, c],
            z_s.at[d],
            z_r.at[1 - d, j],
            {"frame": f - 1 + 2 * d, "height": 2 * y + g},
        )

    def z_arrival(d, j):
        dst = kv.at[2 * d, :, j]
        return remote(dst, dst, z_s.at[d], z_r.at[d, j], partner)

    def z_sent(d):
        src = packed.at[pl.ds(0, 2), pl.ds(0, nf)]
        return remote(src, src, z_s.at[d], z_r.at[d, 0], partner)

    runs = ((nf, h1), (h0, nf))

    def q_copy(d, i, g):
        j, end = part(*runs[i], g)
        return remote(
            packed.at[2, pl.ds(g * HALF + j, end - j)],
            qa.at[pl.ds(j, end - j), 2 - d, c],
            q_s.at[d],
            q_r.at[1 - d, i],
            {"height": 2 * y_dev[d] + g},
        )

    def q_arrival(d, i, g):
        j, end = part(*runs[i], g)
        dst = qa.at[pl.ds(j, end - j), 1 + d]
        return remote(dst, dst, q_s.at[d], q_r.at[d, i], partner)

    def q_sent(d):
        src = packed.at[2, pl.ds(0, nh)]
        return remote(src, src, q_s.at[d], q_r.at[d, 0], partner)

    def filled(i, g):
        j, end = part(*runs[i], g)
        return j < end

    def ret_copy(d, j):
        return remote(
            rs.at[d, j],
            rr.at[1 - d, j],
            ret_s.at[d, j],
            ret_r.at[1 - d, j],
            {"height": 2 * y_dev[d] + c},
        )

    def o_copy(j):
        return remote(oh.at[other, j], out.at[c * HALF + j], o_s, o_r, partner)

    def o_arrivals():
        return remote(oh.at[other], out.at[pl.ds(other * HALF, HALF)], o_s, o_r, partner)

    def o_store(j):
        return pltpu.make_async_copy(oh.at[c, j], out.at[c * HALF + j], o_l)

    def o_stores():
        return pltpu.make_async_copy(oh.at[c], out.at[pl.ds(c * HALF, HALF)], o_l)

    for copy in own_loads:
        copy.start()

    for d in range(2):

        @pl.when(jnp.logical_not(y_ok[d]))
        def _():
            rr[d] = jnp.zeros(rr.shape[1:], rr.dtype)

        @pl.when(jnp.logical_not(z_ok[d]))
        def _():
            kv[2 * d] = jnp.zeros(kv.shape[1:], kv.dtype)

    pl.semaphore_wait(
        barrier,
        1
        + 2 * sum(jnp.where(ok, 1, 0) for ok in z_ok)
        + 2 * sum(jnp.where(ok, 1, 0) for ok in y_ok),
    )

    batches = [[s for s in (2 * j + 1, 2 * j) if s < nf] for j in reversed(range((nf + 1) // 2))]
    window = 2 + nf % 2

    def send_z(d, chosen):
        for slots in chosen:
            for s in slots:
                z_copy(d, s).start()

    @pl.when(has_z(far))
    def _():
        send_z(far, batches[:window])

    @pl.when(has_z(far) & crosses)
    def _():
        send_z(far, batches[window:])

    for copy in own_copies:
        copy.start()

    @pl.when(has_z(near))
    def _():
        send_z(near, batches[:window])

    for i in range(2):
        for d in range(2):

            @pl.when(y_ok[d])
            def _():
                for g in range(2):
                    if filled(i, g):
                        q_copy(d, i, g).start()

    key_side = lax.broadcasted_iota(jnp.int32, (W, 3 * CHIP), 0) // TW
    query_side = lax.broadcasted_iota(jnp.int32, (W, 3 * CHIP), 1) % W // TW
    apart = jnp.where(key_side == query_side, 0.0, NEG).astype(jnp.float32)
    ones = jnp.ones((EXTRA, CHIP), jnp.bfloat16)

    def shut(j, column):
        return (1 - flags[2 * j + c, column]).astype(jnp.float32)

    def keys(tile, j):
        return kv[tile, 0, j].reshape(CHIP, HD)

    def values(tile, j):
        vt = jnp.concatenate([kv[tile, 1, j, 0], kv[tile, 1, j, 1]], axis=1)
        return jnp.concatenate([vt, ones], axis=0)

    def scores(k, j, parts):
        q = qa[j, 0:parts].reshape(parts * CHIP, HD)
        return dot(k, q, ((1,), (1,)))

    def weights(s, m):
        return jnp.exp2((s - m) * SCALE).astype(jnp.bfloat16)

    def here(j, parts):
        n = parts * CHIP
        s = scores(keys(1, j), j, parts)
        bias = apart[:, :n] * shut(j, 2)
        s = (s.reshape(CHIP // W, W, n) + bias[None]).reshape(CHIP, n)
        m = jnp.max(s, axis=0, keepdims=True)
        top[j, 0:1, 0:n] = m
        acc[j, :, 0:n] = dot(values(1, j), weights(s, m), ((1,), (0,)))

    def wait_z(d, j):
        @pl.when(has_z(d))
        def _():
            z_arrival(d, j).wait_recv()

    def around(j, parts):
        n = parts * CHIP
        s = scores(jnp.concatenate([keys(0, j), keys(2, j)], axis=0), j, parts)
        width = apart[:, :n] * shut(j, 2)
        closed = shut(j, 0) * NEG
        bias = jnp.stack([width + jnp.where(z_ok[d], closed, NEG) for d in range(2)])[:, None]
        s = (s.reshape(2, CHIP // W, W, n) + bias).reshape(2 * CHIP, n)
        m_old = top[j, 0:1, 0:n]
        m = jnp.maximum(m_old, jnp.max(s, axis=0, keepdims=True))
        vt = jnp.concatenate([values(0, j), values(2, j)], axis=1)
        fade = jnp.exp2((m_old - m) * SCALE)
        top[j, 0:1, 0:n] = m
        acc[j, :, 0:n] = acc[j, :, 0:n] * fade + dot(vt, weights(s, m), ((1,), (0,)))

    def give_back(j):
        n = slice(CHIP, 3 * CHIP)
        m = top[j, 0:1, n]
        total = acc[j, HD : HD + 1, n]
        o = (acc[j, 0:HD, n] * (1.0 / total)).astype(jnp.bfloat16)
        level = m * SCALE + jnp.log2(total)
        a = level.astype(jnp.bfloat16).astype(jnp.float32)
        b = (level - a).astype(jnp.bfloat16).astype(jnp.float32)
        row = lax.broadcasted_iota(jnp.int32, (EXTRA, 2 * CHIP), 0)
        rest = jnp.where(row == 2, level - a - b, 0.0)
        digits = jnp.where(row == 0, a, jnp.where(row == 1, b, rest)).astype(jnp.bfloat16)
        for d in range(2):
            rs[d, j, 0:HD] = o[:, d * CHIP : (d + 1) * CHIP]
            rs[d, j, HD : HD + EXTRA] = digits[:, d * CHIP : (d + 1) * CHIP]
        for d in range(2):

            @pl.when(y_ok[d])
            def _():
                ret_copy(d, j).start()

    def finish(j, o):
        o = o.T.astype(jnp.bfloat16)
        oh[0, j] = o[:TOK]
        oh[1, j] = o[TOK:]
        o_copy(j).start()
        o_store(j).start()

    def alone(j):
        finish(j, acc[j, 0:HD, 0:CHIP] * (1.0 / acc[j, HD : HD + 1, 0:CHIP]))

    def join(j):
        for d in range(2):

            @pl.when(y_ok[d])
            def _():
                ret_copy(1 - d, j).wait_recv()
                ret_copy(d, j).wait_send()

        m = top[j, 0:1, 0:CHIP] * SCALE
        total = acc[j, HD : HD + 1, 0:CHIP]
        low = shut(j, 1) * NEG
        levels = []
        for d in range(2):
            digits = rr[d, j, HD : HD + EXTRA].astype(jnp.float32)
            level = jnp.sum(digits, axis=0, keepdims=True)
            levels.append(level + jnp.where(y_ok[d], low, NEG))
        best = jnp.maximum(m + jnp.log2(total), jnp.maximum(levels[0], levels[1]))
        w = [jnp.exp2(x - best) for x in (m, *levels)]
        over = 1.0 / (total * w[0] + w[1] + w[2])
        o = acc[j, 0:HD, 0:CHIP] * (w[0] * over)
        for d in range(2):
            o = o + rr[d, j, 0:HD].astype(jnp.float32) * (w[d + 1] * over)
        finish(j, o)

    for copy in own_loads:
        copy.wait()
    for copy in own_copies:
        copy.wait_recv()

    lo, hi = part(h0, h1, c)
    my_z = part(0, nf, c)[1]
    n_in = my_z - lo
    n_out = hi - my_z

    @pl.loop(0, lo + HALF - hi)
    def _(n):
        j = jnp.where(n < lo, n, n - lo + hi)
        here(j, 1)

        @pl.when(j >= hi)
        def _():
            alone(j)

    @pl.loop(0, n_out + n_in)
    def _(n):
        j = jnp.where(n < n_out, my_z + n, my_z - 1 - (n - n_out))
        for i in range(2):
            for d in range(2):
                for g in range(2):
                    if filled(i, g):

                        @pl.when((n == (n_out if i else 0)) & (c == g) & y_ok[d])
                        def _():
                            q_arrival(d, i, g).wait_recv()

        here(j, 3)

        @pl.when(n < n_out)
        def _():
            give_back(j)

    @pl.when(has_z(near))
    def _():
        send_z(near, batches[window:])

    @pl.when(has_z(far) & jnp.logical_not(crosses))
    def _():
        send_z(far, batches[window:])

    @pl.loop(my_z, hi)
    def _(j):
        join(j)

    @pl.loop(0, n_in)
    def _(n):
        j = my_z - 1 - n
        for d in (near, far):
            wait_z(d, j)
        around(j, 3)
        give_back(j)

    @pl.loop(0, n_in)
    def _(n):
        join(my_z - 1 - n)

    if h0 > 0:

        @pl.loop(0, lo)
        def _(i):
            j = lo - 1 - i
            wait_z(near, j)
            wait_z(far, j)
            around(j, 1)
            alone(j)

    for copy in own_copies:
        copy.wait_send()
    for d in range(2):

        @pl.when(z_ok[d])
        def _():
            z_sent(d).wait_send()

        @pl.when(y_ok[d])
        def _():
            q_sent(d).wait_send()

    o_stores().wait()
    o_arrivals().wait()


def attend(index, n_frame, n_chip_y, packed, flags):
    nf, nh, both = PLANS[index]
    assert both <= min(nf, nh) and nf + nh - both <= HEADS
    bf16, f32 = jnp.bfloat16, jnp.float32
    dma = pltpu.SemaphoreType.DMA
    return pl.pallas_call(
        functools.partial(kernel, PLANS[index], n_frame, n_chip_y),
        out_shape=jax.ShapeDtypeStruct((HEADS, TOK, HD), bf16),
        in_specs=[pl.BlockSpec(memory_space=pl.ANY), pl.BlockSpec(memory_space=pltpu.SMEM)],
        out_specs=pl.BlockSpec(memory_space=pl.ANY),
        scratch_shapes=[
            pltpu.VMEM((3, 2, HALF, 2, TOK, HD), bf16),
            pltpu.VMEM((HALF, 3, 2, TOK, HD), bf16),
            pltpu.VMEM((HALF, HD + EXTRA, 3 * CHIP), f32),
            pltpu.VMEM((HALF, 8, 3 * CHIP), f32),
            pltpu.VMEM((2, HALF, HD + EXTRA, CHIP), bf16),
            pltpu.VMEM((2, HALF, HD + EXTRA, CHIP), bf16),
            pltpu.VMEM((2, HALF, TOK, HD), bf16),
            dma((2,)),
            dma((2,)),
            dma((2,)),
            dma((2,)),
            dma((2, HALF)),
            dma((2,)),
            dma((2, 2)),
            dma((2, HALF)),
            dma((2, HALF)),
            dma,
            dma,
            dma,
        ],
        compiler_params=pltpu.CompilerParams(
            collective_id=index,
            has_side_effects=True,
            vmem_limit_bytes=32 * 1024 * 1024,
        ),
    )(packed, flags)


def shards(queries, key_value, windows):
    n_frame = lax.axis_size("frame")
    n_chip_y = lax.axis_size("height") // 2
    width = HEADS * HD
    vmem = pl.BlockSpec(memory_space=pltpu.VMEM)
    smem = pl.BlockSpec(memory_space=pltpu.SMEM)
    packed, flags, choice = pl.pallas_call(
        sort_kernel,
        out_shape=(
            jax.ShapeDtypeStruct((3, HEADS, TOK, HD), jnp.bfloat16),
            jax.ShapeDtypeStruct((HEADS, 4), jnp.int32),
            jax.ShapeDtypeStruct((1,), jnp.int32),
        ),
        in_specs=[vmem, vmem, smem],
        out_specs=(vmem, smem, smem),
    )(queries.reshape(TOK, width), key_value.reshape(2, TOK, width), windows.T)
    branches = [functools.partial(attend, i, n_frame, n_chip_y) for i in range(len(PLANS))]
    slots = lax.switch(choice[0], branches, packed, flags)
    result = pl.pallas_call(
        place_kernel,
        out_shape=jax.ShapeDtypeStruct((TOK, width), jnp.bfloat16),
        in_specs=[vmem, smem],
        out_specs=vmem,
    )(slots, flags)
    return result.reshape(queries.shape)


def solution(mesh):
    in_specs = (
        P(("cand", "frame"), "height", None, None),
        P(None, ("cand", "frame"), "height", None, None),
        P(),
    )
    out_specs = P(("cand", "frame"), "height", None, None)
    return jax.shard_map(shards, mesh=mesh, in_specs=in_specs, out_specs=out_specs, check_vma=False)
```
